512 devices in a mesh: grp: 32 (over z_lo, y, core), sub: 16 (over z_hi, x).
Axes of the slice: x: 4, y: 4, z: 16 (z_hi: 4, z_lo: 4; z = z_hi * 4 + z_lo), core: 2. Of those that a mesh axis runs over, the one named last changes fastest.
Arguments:
- coeffs: bfloat16 [64, 240, 8192], P('grp', None, 'sub'), may hold values from -0.0625 to 0.0625
- offsets: bfloat16 [64, 3, 8192], P('grp', None, 'sub'), may hold values from -6 to 6
- moments: bfloat16 [64, 3, 8192], P('grp', None, 'sub'), may hold values from -6 to 6
- centers: float32 [64, 3], replicated, may hold values from -40 to 40
- near_flags: int32 [64, 64], replicated, may hold values from 0 to 1, as said below
- lobe_weights: float32 [1440], P('sub'), may hold values from 0.3 to 3
- near_boost: float32 [1440], P('sub'), may hold values from 0.5 to 2
Outputs:
- lower_coupling: float32 [64, 2, 2, 240, 240], P('grp', None, None, None, 'sub')
- upper_coupling: float32 [64, 2, 2, 240, 240], P('grp', None, None, 'sub')
The draws below stay inside these ranges and needn't reach their ends.
Inputs may be any that keep to these rules, and one draw needn't show every extreme that they name: near_flags is symmetric: near_flags[m, n] equals near_flags[n, m].
All inputs are finite; a program needn't handle non-finite values.
Results may differ from the reference program's by a relative error of at most 0.02.
Values may be sent and summed in bfloat16 or wider, within the bound.
A program may use at most 64 MiB of HBM per device.

```python
import math
import jax
import jax.numpy as jnp
from jax import lax

UNKNOWN_TOTAL = 8192
BASIS_PER_BLOCK = 240
THETAS = 20
PHIS = 36
DIRS = 720
LOBE_TOTAL = 1440
BLOCKS_IN_GROUP = 2
ROUND_TOTAL = 2
BLOCK_TOTAL = 64
N_GRP = 32


def draw_near_flags(key, part):
    key = jax.random.fold_in(key, 7)
    raw = jax.random.randint(key, (BLOCK_TOTAL, BLOCK_TOTAL), 0, 2)
    rows = jnp.arange(BLOCK_TOTAL)[:, None]
    columns = jnp.arange(BLOCK_TOTAL)[None, :]
    return jnp.where(rows <= columns, raw, raw.T).astype(jnp.int32)


def block_levels(key, dims, cuts, low, largest):
    def one(dim, blocks):
        heights = jax.random.uniform(jax.random.fold_in(jax.random.fold_in(key, 6), dim), (blocks,), jnp.float32, low / len(cuts), largest / len(cuts))
        return jnp.repeat(jnp.exp(heights), dims[dim] // blocks).reshape((-1,) + (1,) * (len(dims) - dim - 1))

    gain = one(*cuts[0])
    for cut in cuts[1:]:
        gain = gain * one(*cut)
    return gain


def gaussian(stream_key, extent, scale, limit, cuts=(), held_as=jnp.bfloat16):
    drawn = scale * jax.random.normal(stream_key, extent, jnp.float32)
    if cuts:
        drawn = drawn * block_levels(stream_key, extent, cuts, -0.22, 0.18)
    return jnp.clip(drawn, -limit, limit).astype(held_as)


def setup_inputs(seed: int = 0) -> dict:
    arg_keys = jax.random.split(jax.random.key(seed), 8)
    coeffs = gaussian(arg_keys[0], (BLOCK_TOTAL, BASIS_PER_BLOCK, UNKNOWN_TOTAL), UNKNOWN_TOTAL ** -0.5, 0.0625, ((0, 32), (2, 16)))
    offsets = jnp.clip(jax.random.uniform(arg_keys[1], (BLOCK_TOTAL, 3, UNKNOWN_TOTAL), jnp.float32, -6.0, 6.0) * block_levels(arg_keys[1], (BLOCK_TOTAL, 3, UNKNOWN_TOTAL), ((0, 32), (2, 16)), -0.4, 0.0), -6.0, 6.0).astype(jnp.bfloat16)
    moments = gaussian(arg_keys[2], (BLOCK_TOTAL, 3, UNKNOWN_TOTAL), 1.0, 6.0, ((0, 32), (2, 16)))
    centers = jnp.clip(jax.random.uniform(arg_keys[3], (BLOCK_TOTAL, 3), jnp.float32, -40.0, 40.0), -40.0, 40.0)
    near_flags = draw_near_flags(jax.random.fold_in(arg_keys[7], 71), 0)
    lobe_weights = jnp.clip(jnp.exp(math.log(3.0) - 2.3025851 * jax.random.uniform(arg_keys[5], (LOBE_TOTAL,), jnp.float32) ** block_levels(arg_keys[5], (LOBE_TOTAL,), ((0, 16),), -0.2, 0.2)), 0.3, 3.0)
    near_boost = jnp.clip(jnp.exp(math.log(2.0) - 1.3862944 * jax.random.uniform(arg_keys[6], (LOBE_TOTAL,), jnp.float32) ** block_levels(arg_keys[6], (LOBE_TOTAL,), ((0, 16),), -0.2, 0.2)), 0.5, 2.0)
    return {"coeffs": coeffs, "offsets": offsets, "moments": moments, "centers": centers, "near_flags": near_flags, "lobe_weights": lobe_weights, "near_boost": near_boost}


wave_number = math.pi
highest = lax.Precision.HIGHEST

def lobe_vectors(lobe_ids):
    polar = lobe_ids // DIRS
    place = lobe_ids % DIRS
    theta = math.pi * ((place // PHIS).astype(jnp.float32) + 0.5) / THETAS
    azimuth = 2.0 * math.pi * (place % PHIS).astype(jnp.float32) / PHIS
    sin_theta = jnp.sin(theta)
    cos_theta = jnp.cos(theta)
    sin_azimuth = jnp.sin(azimuth)
    cos_azimuth = jnp.cos(azimuth)
    heading = jnp.stack([sin_theta * cos_azimuth, sin_theta * sin_azimuth, cos_theta])
    along_theta = jnp.stack([cos_theta * cos_azimuth, cos_theta * sin_azimuth, -sin_theta])
    along_phi = jnp.stack([-sin_azimuth, cos_azimuth, jnp.zeros_like(sin_azimuth)])
    field = jnp.where((polar == 0)[None, :], along_theta, along_phi)
    return (heading, field)

def samples(heading, field, offsets, moments):
    phase = wave_number * jnp.einsum('cl,bcu->blu', heading, offsets.astype(jnp.float32), precision=highest)
    weight = jnp.einsum('cl,bcu->blu', field, moments.astype(jnp.float32), precision=highest)
    return jnp.stack([weight * jnp.cos(phase), -weight * jnp.sin(phase)], axis=1).astype(jnp.bfloat16)

def couple(mine, theirs, mine_centers, their_centers, flags, heading, weights, boost):
    along_mine = jnp.einsum('ic,cl->il', mine_centers, heading, precision=highest)
    along_theirs = jnp.einsum('jc,cl->jl', their_centers, heading, precision=highest)
    angle = wave_number * (along_mine[:, None, :] - along_theirs[None, :, :])
    amplitude = (weights[None, None, :] + flags[:, :, None].astype(jnp.float32) * boost[None, None, :]) / math.sqrt(LOBE_TOTAL)
    cosine = (amplitude * jnp.cos(angle))[..., None]
    sine = (amplitude * jnp.sin(angle))[..., None]
    left = mine.astype(jnp.float32)
    right = theirs.astype(jnp.float32)
    real_part = right[:, 0][None]
    imag_part = right[:, 1][None]
    carry_real = (cosine * real_part - sine * imag_part).astype(jnp.bfloat16).astype(jnp.float32)
    carry_imag = (sine * real_part + cosine * imag_part).astype(jnp.bfloat16).astype(jnp.float32)
    first = jnp.einsum('ila,ijlb->ijab', left[:, 0], carry_real, precision=highest)
    second = jnp.einsum('ila,ijlb->ijab', left[:, 1], carry_imag, precision=highest)
    return first + second

def reference(coeffs, offsets, moments, centers, near_flags, lobe_weights, near_boost):
    heading, field = lobe_vectors(jnp.arange(LOBE_TOTAL, dtype=jnp.int32))

    def project(item):
        basis_weight, offset, moment = item
        sample_draw = samples(heading, field, offset[None], moment[None])[0]
        lobe_totals = jnp.einsum('evj,aj->eva', sample_draw.astype(jnp.float32), basis_weight.astype(jnp.float32))
        return lobe_totals.astype(jnp.bfloat16)
    wave_patterns = lax.map(project, (coeffs, offsets, moments))
    group_sorted = wave_patterns.reshape(N_GRP, BLOCKS_IN_GROUP, 2, LOBE_TOTAL, BASIS_PER_BLOCK)
    spots = centers.reshape(N_GRP, BLOCKS_IN_GROUP, 3)
    flags_table = near_flags.reshape(N_GRP, BLOCKS_IN_GROUP, N_GRP, BLOCKS_IN_GROUP)
    groups = jnp.arange(N_GRP, dtype=jnp.int32)
    lower_group = []
    upper_group = []
    for shift_by in range(1, ROUND_TOTAL + 1):
        partner = (groups - shift_by) % N_GRP
        pair_flags = flags_table[groups, :, partner, :]

        def one_group(item):
            mine, theirs, mine_spots, their_spots, flags = item
            return couple(mine, theirs, mine_spots, their_spots, flags, heading, lobe_weights, near_boost)
        coupled = lax.map(one_group, (group_sorted, group_sorted[partner], spots, spots[partner], pair_flags))
        lower_group.append(coupled)
        upper_group.append(jnp.transpose(jnp.roll(coupled, -shift_by, axis=0), (0, 2, 1, 4, 3)))
    lower_coupling = jnp.stack(lower_group, axis=2).reshape(BLOCK_TOTAL, ROUND_TOTAL, BLOCKS_IN_GROUP, BASIS_PER_BLOCK, BASIS_PER_BLOCK)
    upper_coupling = jnp.stack(upper_group, axis=2).reshape(BLOCK_TOTAL, ROUND_TOTAL, BLOCKS_IN_GROUP, BASIS_PER_BLOCK, BASIS_PER_BLOCK)
    return (lower_coupling, upper_coupling)
```

```python
import math

import jax
import jax.numpy as jnp
import numpy as np
from jax import lax
from jax.experimental import pallas as pl
from jax.experimental.pallas import tpu as pltpu
from jax.sharding import PartitionSpec as P

THETAS = 20
PHIS = 36
DIRS = 720
LOBE_TOTAL = 1440
ROUND_TOTAL = 2
BASIS = 240
RING = 4
HALF = 45
ROWS = 48
SLAB = 15
LANES = 256
DEPTH = 32
MESH = pl.DeviceIdType.MESH


def heading_of(t):
    theta = np.pi * ((t // PHIS) + 0.5) / THETAS
    azimuth = 2.0 * np.pi * (t % PHIS) / PHIS
    st, ct, sa, ca = np.sin(theta), np.cos(theta), np.sin(azimuth), np.cos(azimuth)
    heading = np.stack([st * ca, st * sa, ct], axis=-1)
    along_theta = np.stack([ct * ca, ct * sa, -st], axis=-1)
    along_phi = np.stack([-sa, ca, np.zeros_like(sa)], axis=-1)
    return heading, along_theta, along_phi


def split3(value):
    value = value.astype(np.float32)
    parts = []
    for _ in range(3):
        part = value.astype(jnp.bfloat16)
        parts.append(part)
        value = value - part.astype(np.float32)
    return np.concatenate(parts, axis=-1)


def grid_tables():
    pieces = np.zeros((RING, 3, 2, ROWS, DEPTH), jnp.bfloat16)
    headings = np.zeros((2 * RING, ROWS, 8), np.float32)
    places = np.full((2 * RING, ROWS, 8), -1, np.int32)
    for xo in range(RING):
        for dh in range(2):
            t = 90 * xo + HALF * dh + np.arange(HALF)
            heading, along_theta, along_phi = heading_of(t)
            pieces[xo, 0, dh, :HALF, 0:9] = split3(0.5 * heading)
            pieces[xo, 1, dh, :HALF, 9:18] = split3(along_theta)
            pieces[xo, 2, dh, :HALF, 9:18] = split3(along_phi)
            headings[2 * xo + dh, :HALF, 0:3] = 0.5 * heading
            opposite = PHIS * (THETAS - 1 - t // PHIS) + (t % PHIS + PHIS // 2) % PHIS
            places[2 * xo + dh, :HALF, 0] = t - 90 * xo
            places[2 * xo + dh, :HALF, 1] = opposite - 90 * (7 - xo)
            assert places[2 * xo + dh, :HALF].min(axis=0)[1] >= 0
            assert places[2 * xo + dh, :HALF].max(axis=0)[1] < 90
    return pieces.reshape(RING, 6 * ROWS, DEPTH), headings, places


def slab_matrix():
    matrix = np.zeros((LANES, LANES), jnp.bfloat16)
    for x in range(RING):
        for z in range(RING):
            for i in range(SLAB):
                matrix[(x * RING + z) * 16 + i, SLAB * (z * RING + x) + i] = 1
    return matrix


def turn_coefficients():
    nodes = np.cos(np.pi * (np.arange(400) + 0.5) / 400)
    square = 0.125 * (nodes + 1.0)
    r = np.sqrt(square)
    fit = np.polynomial.chebyshev.Chebyshev.fit
    cosine = fit(square, np.cos(2 * np.pi * r), 6, domain=[0, 0.25])
    sine = fit(square, -np.sin(2 * np.pi * r) / r, 5, domain=[0, 0.25])
    convert = np.polynomial.polynomial.Polynomial
    return (
        [float(v) for v in cosine.convert(kind=convert, domain=[-1, 1]).coef],
        [float(v) for v in sine.convert(kind=convert, domain=[-1, 1]).coef],
    )


COS_TERMS, SIN_TERMS = turn_coefficients()


def turn(s):
    r = s - jnp.round(s)
    y = r * r
    cosine = jnp.full_like(y, COS_TERMS[-1])
    for term in COS_TERMS[-2::-1]:
        cosine = cosine * y + term
    sine = jnp.full_like(y, SIN_TERMS[-1])
    for term in SIN_TERMS[-2::-1]:
        sine = sine * y + term
    return cosine, sine * r


def rounded(value):
    return value.astype(jnp.bfloat16)


def wide(value):
    return value.astype(jnp.float32)


class Copies:
    def __init__(self, send_sems, recv_sems):
        self.send_sems, self.recv_sems = send_sems, recv_sems
        self.all = []

    def start(self, source, target, device):
        place = len(self.all)
        copy = pltpu.make_async_remote_copy(
            src_ref=source,
            dst_ref=target,
            send_sem=self.send_sems.at[place],
            recv_sem=self.recv_sems.at[place],
            device_id=device,
            device_id_type=MESH,
        )
        copy.start()
        self.all.append(copy)
        return copy

    def finish(self):
        for copy in self.all:
            copy.wait_send()


class Ring:
    def __init__(self, copies, me, left, right, source, first, second, near, far):
        self.copies, self.left, self.right = copies, left, right
        self.across = source(lax.rem(me + 2, RING))
        self.after = source(lax.rem(me + 1, RING))
        self.before = source(lax.rem(me + 3, RING))
        self.own = source(me)
        self.first, self.second, self.near, self.far = first, second, near, far

    def step_1(self):
        self.from_left = self.copies.start(self.across.at[self.first], self.near.at[0], self.right)
        self.from_right = self.copies.start(self.across.at[self.second], self.near.at[1], self.left)

    def step_2(self):
        self.from_left.wait_recv()
        half = self.after.at[self.first]
        half[...] = rounded(wide(half[...]) + wide(self.near[0]))
        from_left = self.copies.start(self.after, self.far.at[0], self.right)
        self.from_right.wait_recv()
        half = self.before.at[self.second]
        half[...] = rounded(wide(half[...]) + wide(self.near[1]))
        from_right = self.copies.start(self.before, self.far.at[1], self.left)
        self.from_left, self.from_right = from_left, from_right

    def total(self):
        self.from_left.wait_recv()
        self.from_right.wait_recv()
        return wide(self.own[...]) + wide(self.far[0]) + wide(self.far[1])


N_COPIES = 3 + 2 * 2 * 4 + 4 + 2 * 2 * 4 + 2


def kernel(
    coeffs_ref, offsets_ref, moments_ref, centers_ref, flags_ref, weights_ref, boost_ref,
    pieces_ref, headings_ref, places_ref, slabs_ref,
    lower_ref, upper_ref,
    geometry, coeffs_pad, turned, samples, part, x_near, x_far, z_send, z_near, z_far,
    patterns, plain, theirs, lobe_send, lobe_recv,
    zp, zx_near, zx_far, zz_send, zz_near, zz_far, up_send, up_recv,
    send_sems, recv_sems,
):
    group = lax.axis_index("grp")
    groups = lax.axis_size("grp")
    sub = lax.axis_index("sub")
    x, z = lax.rem(sub, RING), sub // RING
    z_odd = lax.rem(z, 2)
    z_pair = z + 1 - 2 * z_odd

    def at(z_to, x_to):
        return {"sub": z_to * RING + x_to}

    x_right, x_left = at(z, lax.rem(x + 1, RING)), at(z, lax.rem(x + 3, RING))
    z_right, z_left = at(lax.rem(z + 1, RING), x), at(lax.rem(z + 3, RING), x)
    corner = at(z_pair, 3 - x)

    def other(shift):
        return {"grp": lax.rem(group + shift + groups, groups)}

    barrier = pltpu.get_barrier_semaphore()
    peers = [x_right, x_left, z_right, z_left, corner, other(1), other(-1), other(2), other(-2)]
    for peer in peers:
        pl.semaphore_signal(barrier, inc=1, device_id=peer, device_id_type=MESH)

    copies = Copies(send_sems, recv_sems)

    for block in range(2):
        geometry[block] = jnp.zeros((DEPTH, geometry.shape[2]), jnp.float32)
        for axis in range(3):
            offset = wide(offsets_ref[axis])[block : block + 1]
            moment = wide(moments_ref[axis])[block : block + 1]
            for piece in range(3):
                geometry[block, 3 * piece + axis : 3 * piece + axis + 1, :] = offset
                geometry[block, 9 + 3 * piece + axis : 10 + 3 * piece + axis, :] = moment
        coeffs_pad[block] = rounded(
            jnp.dot(slabs_ref[:, :BASIS], coeffs_ref[block], preferred_element_type=jnp.float32)
        )
    lobe_send[...] = jnp.zeros_like(lobe_send)
    lobe_send[0:1, 0 : weights_ref.shape[1]] = weights_ref[...]
    lobe_send[1:2, 0 : weights_ref.shape[1]] = boost_ref[...]

    def project(owner, block):
        turned[...] = jnp.dot(
            pieces_ref[owner], rounded(geometry[block]), preferred_element_type=jnp.float32
        )

        def rows_of(step, carried):
            low = pl.multiple_of(step * 16, 16)
            half, inner = step // 3, pl.multiple_of(lax.rem(step, 3) * 16, 16)
            cosine, sine = turn(turned[pl.ds(low, 16), :])
            for polar in range(2):
                weight = turned[pl.ds(low + (polar + 1) * 2 * ROWS, 16), :]
                samples[polar * 2 + half, 0, pl.ds(inner, 16), :] = rounded(weight * cosine)
                samples[polar * 2 + half, 1, pl.ds(inner, 16), :] = rounded(weight * sine)
            return carried

        lax.fori_loop(0, 6, rows_of, 0)
        sums = lax.dot_general(
            samples[...].reshape(8 * ROWS, samples.shape[3]),
            coeffs_pad[block],
            (((1,), (1,)), ((), ())),
            preferred_element_type=jnp.float32,
        )
        part[owner, block] = rounded(sums).reshape(4, 2, ROWS, LANES)

    across, after, before = lax.rem(x + 2, RING), lax.rem(x + 1, RING), lax.rem(x + 3, RING)
    x_rings = [
        Ring(
            copies, x, x_left, x_right, lambda o, b=b: part.at[o, b],
            pl.ds(0, 2), pl.ds(2, 2), x_near.at[b], x_far.at[b],
        )
        for b in range(2)
    ]
    z_rings = [
        Ring(
            copies, z, z_left, z_right, lambda o, b=b: z_send.at[b, o],
            0, 1, z_near.at[b], z_far.at[b],
        )
        for b in range(2)
    ]

    project(across, 0)
    pl.semaphore_wait(barrier, len(peers))
    x_rings[0].step_1()
    lobes = [
        copies.start(lobe_send, lobe_recv.at[k], peer)
        for k, peer in enumerate([at(z_pair, x), at(z, 3 - x), corner])
    ]
    project(across, 1)
    x_rings[1].step_1()
    project(after, 0)
    project(before, 0)
    x_rings[0].step_2()
    project(after, 1)
    project(before, 1)
    x_rings[1].step_2()
    project(x, 0)
    z_send[0] = rounded(x_rings[0].total())
    z_rings[0].step_1()
    project(x, 1)
    z_rings[0].step_2()
    z_send[1] = rounded(x_rings[1].total())
    z_rings[1].step_1()

    to_groups = []

    def settle(block):
        patterns[block] = rounded(z_rings[block].total())
        for r in range(ROUND_TOTAL):
            to_groups.append(copies.start(patterns.at[block], theirs.at[r, block], other(r + 1)))
        plain[block] = rounded(
            jnp.dot(
                patterns[block].reshape(2 * ROWS, LANES), slabs_ref[...], preferred_element_type=jnp.float32
            )
        )

    settle(0)
    z_rings[1].step_2()

    for lobe in lobes:
        lobe.wait_recv()
    odd = z_odd.astype(jnp.float32)
    lane = lax.broadcasted_iota(jnp.int32, (ROWS, 128), 1)
    place = places_ref[x * 2 + z_odd]
    heading = headings_ref[x * 2 + z_odd]

    def lobe_column(row):
        near = lobe_send[row : row + 1, :] * (1.0 - odd) + lobe_recv[0, row : row + 1, :] * odd
        far = lobe_recv[2, row : row + 1, :] * (1.0 - odd) + lobe_recv[1, row : row + 1, :] * odd
        picked = jnp.where(lane == place[:, 0:1], near, 0.0) + jnp.where(lane == place[:, 1:2], far, 0.0)
        return jnp.sum(picked, axis=1, keepdims=True)

    weight_sum, boost_sum = lobe_column(0), lobe_column(1)
    pair_lane = lax.broadcasted_iota(jnp.int32, (1, 128), 1)
    flag_row = jnp.zeros((1, 128), jnp.float32)
    offset_rows = [jnp.zeros((1, 128), jnp.float32) for _ in range(3)]
    for r in range(ROUND_TOTAL):
        partner = lax.rem(group - r - 1 + groups, groups)
        for i in range(2):
            for j in range(2):
                m, n = group * 2 + i, partner * 2 + j
                here = pair_lane == (r * 4 + i * 2 + j)
                flag_row = jnp.where(here, flags_ref[m, n].astype(jnp.float32), flag_row)
                for axis in range(3):
                    gap = centers_ref[axis, m] - centers_ref[axis, n]
                    offset_rows[axis] = jnp.where(here, gap, offset_rows[axis])
    cosine, sine = turn(
        heading[:, 0:1] * offset_rows[0] + heading[:, 1:2] * offset_rows[1] + heading[:, 2:3] * offset_rows[2]
    )
    amplitude = (weight_sum + flag_row * boost_sum) * (1.0 / math.sqrt(LOBE_TOTAL))
    cosine, sine = amplitude * cosine, amplitude * sine

    zx_rings = [
        Ring(
            copies, x, x_left, x_right, lambda o, r=r: zp.at[o, r],
            pl.ds(0, 2), pl.ds(2, 2), zx_near.at[r], zx_far.at[r],
        )
        for r in range(ROUND_TOTAL)
    ]
    zz_rings = [
        Ring(
            copies, z, z_left, z_right, lambda o, r=r: zz_send.at[r, o],
            pl.ds(0, 2), pl.ds(2, 2), zz_near.at[r], zz_far.at[r],
        )
        for r in range(ROUND_TOTAL)
    ]
    settle(1)

    for r in range(ROUND_TOTAL):
        for j in range(2):
            to_groups[2 * j + r].wait_recv()
            real, imag = wide(theirs[r, j, 0]), wide(theirs[r, j, 1])
            for i in range(2):
                pair = i * 2 + j
                lane_at = r * 4 + pair
                c, s = cosine[:, lane_at : lane_at + 1], sine[:, lane_at : lane_at + 1]
                carry = jnp.concatenate([rounded(c * real + s * imag), rounded(c * imag - s * real)], axis=0)
                z_part = rounded(
                    lax.dot_general(
                        carry, plain[i], (((0,), (0,)), ((), ())), preferred_element_type=jnp.float32
                    )
                )
                for to_x in range(RING):
                    for to_z in range(RING):
                        low = (to_x * RING + to_z) * 16
                        zp[to_x, r, to_z, pair] = z_part[low : low + 16]
        zx_rings[r].step_1()

    zx_rings[0].step_2()
    zx_rings[1].step_2()
    zz_send[0] = rounded(zx_rings[0].total())
    zz_rings[0].step_1()
    zz_send[1] = rounded(zx_rings[1].total())
    zz_rings[1].step_1()
    zz_rings[0].step_2()
    zz_rings[1].step_2()

    back = []
    for r in range(ROUND_TOTAL):
        total = zz_rings[r].total()
        up_send[r] = rounded(total)
        back.append(copies.start(up_send.at[r], up_recv.at[r], other(-r - 1)))
        for i in range(2):
            for j in range(2):
                lower_ref[i, r, :, j, :] = total[i * 2 + j, :SLAB, :BASIS]
    for r in range(ROUND_TOTAL):
        back[r].wait_recv()
        for i in range(2):
            for j in range(2):
                upper_ref[j, r, :, i, :] = wide(up_recv[r, i * 2 + j])[:SLAB, :BASIS]
    copies.finish()


def shards(coeffs, offsets, moments, centers, near_flags, lobe_weights, near_boost):
    pieces, headings, places = grid_tables()
    unknowns = coeffs.shape[2]
    bf16, f32 = jnp.bfloat16, jnp.float32
    vmem = pl.BlockSpec(memory_space=pltpu.VMEM)
    smem = pl.BlockSpec(memory_space=pltpu.SMEM)
    out = jax.ShapeDtypeStruct((2, ROUND_TOTAL, SLAB, 2, BASIS), f32)
    lower, upper = pl.pallas_call(
        kernel,
        out_shape=(out, out),
        in_specs=[vmem, vmem, vmem, smem, smem, vmem, vmem, vmem, vmem, vmem, vmem],
        out_specs=(vmem, vmem),
        scratch_shapes=[
            pltpu.VMEM((2, DEPTH, unknowns), f32),
            pltpu.VMEM((2, LANES, unknowns), bf16),
            pltpu.VMEM((6 * ROWS, unknowns), f32),
            pltpu.VMEM((4, 2, ROWS, unknowns), bf16),
            pltpu.VMEM((RING, 2, RING, 2, ROWS, LANES), bf16),
            pltpu.VMEM((2, 2, 2, 2, ROWS, LANES), bf16),
            pltpu.VMEM((2, 2, RING, 2, ROWS, LANES), bf16),
            pltpu.VMEM((2, RING, 2, ROWS, LANES), bf16),
            pltpu.VMEM((2, 2, ROWS, LANES), bf16),
            pltpu.VMEM((2, 2, 2, ROWS, LANES), bf16),
            pltpu.VMEM((2, 2, ROWS, LANES), bf16),
            pltpu.VMEM((2, 2 * ROWS, LANES), bf16),
            pltpu.VMEM((ROUND_TOTAL, 2, 2, ROWS, LANES), bf16),
            pltpu.VMEM((8, 128), f32),
            pltpu.VMEM((3, 8, 128), f32),
            pltpu.VMEM((RING, ROUND_TOTAL, RING, 4, 16, LANES), bf16),
            pltpu.VMEM((ROUND_TOTAL, 2, 2, 4, 16, LANES), bf16),
            pltpu.VMEM((ROUND_TOTAL, 2, RING, 4, 16, LANES), bf16),
            pltpu.VMEM((ROUND_TOTAL, RING, 4, 16, LANES), bf16),
            pltpu.VMEM((ROUND_TOTAL, 2, 2, 16, LANES), bf16),
            pltpu.VMEM((ROUND_TOTAL, 2, 4, 16, LANES), bf16),
            pltpu.VMEM((ROUND_TOTAL, 4, 16, LANES), bf16),
            pltpu.VMEM((ROUND_TOTAL, 4, 16, LANES), bf16),
            pltpu.SemaphoreType.DMA((N_COPIES,)),
            pltpu.SemaphoreType.DMA((N_COPIES,)),
        ],
        compiler_params=pltpu.CompilerParams(
            collective_id=0, has_side_effects=True, vmem_limit_bytes=40 * 1024 * 1024
        ),
        name="fill",
    )(
        coeffs,
        jnp.transpose(offsets, (1, 0, 2)),
        jnp.transpose(moments, (1, 0, 2)),
        jnp.transpose(centers),
        near_flags,
        lobe_weights.reshape(1, -1),
        near_boost.reshape(1, -1),
        jnp.asarray(pieces),
        jnp.asarray(headings),
        jnp.asarray(places),
        jnp.asarray(slab_matrix()),
    )
    return jnp.transpose(lower, (0, 1, 3, 4, 2)), jnp.transpose(upper, (0, 1, 3, 2, 4))


def solution(mesh):
    placed = (
        P("grp", None, "sub"),
        P("grp", None, "sub"),
        P("grp", None, "sub"),
        P(),
        P(),
        P("sub"),
        P("sub"),
    )
    return jax.shard_map(
        shards,
        mesh=mesh,
        in_specs=placed,
        out_specs=(P("grp", None, None, None, "sub"), P("grp", None, None, "sub", None)),
        check_vma=False,
    )
```

```python
import math

import jax
import jax.numpy as jnp
import numpy as np
from jax import lax
from jax.experimental import pallas as pl
from jax.experimental.pallas import tpu as pltpu
from jax.sharding import PartitionSpec as P

THETAS = 20
PHIS = 36
DIRS = 720
LOBE_TOTAL = 1440
ROUND_TOTAL = 2
BASIS = 240
RING = 4
HALF = 45
ROWS = 48
HOLD = 64
SLAB = 15
LANES = 256
DEPTH = 32
MESH = pl.DeviceIdType.MESH


def heading_of(t):
    theta = np.pi * ((t // PHIS) + 0.5) / THETAS
    azimuth = 2.0 * np.pi * (t % PHIS) / PHIS
    st, ct, sa, ca = np.sin(theta), np.cos(theta), np.sin(azimuth), np.cos(azimuth)
    heading = np.stack([st * ca, st * sa, ct], axis=-1)
    along_theta = np.stack([ct * ca, ct * sa, -st], axis=-1)
    along_phi = np.stack([-sa, ca, np.zeros_like(sa)], axis=-1)
    return heading, along_theta, along_phi


def split3(value):
    value = value.astype(np.float32)
    parts = []
    for _ in range(3):
        part = value.astype(jnp.bfloat16)
        parts.append(part)
        value = value - part.astype(np.float32)
    return np.concatenate(parts, axis=-1)


def grid_tables():
    pieces = np.zeros((RING, 3, 2, ROWS, DEPTH), jnp.bfloat16)
    headings = np.zeros((2 * RING, 8, 2, HOLD), np.float32)
    places = np.full((2 * RING, 8, 2, HOLD), -1, np.int32)
    for xo in range(RING):
        for dh in range(2):
            t = 90 * xo + HALF * dh + np.arange(HALF)
            heading, along_theta, along_phi = heading_of(t)
            pieces[xo, 0, dh, :HALF, 0:9] = split3(0.5 * heading)
            pieces[xo, 1, dh, :HALF, 9:18] = split3(along_theta)
            pieces[xo, 2, dh, :HALF, 9:18] = split3(along_phi)
            headings[2 * xo + dh, 0:3, :, :HALF] = 0.5 * heading.T[:, None]
            opposite = PHIS * (THETAS - 1 - t // PHIS) + (t % PHIS + PHIS // 2) % PHIS - 90 * (7 - xo)
            assert opposite.min() >= 0 and opposite.max() < 90
            places[2 * xo + dh, 0, :, :HALF] = t - 90 * xo
            places[2 * xo + dh, 1, :, :HALF] = opposite
    wide_as = (2 * RING, 8, 2 * HOLD)
    return pieces.reshape(RING, 6 * ROWS, DEPTH), headings.reshape(wide_as), places.reshape(wide_as)


def turn_coefficients():
    nodes = np.cos(np.pi * (np.arange(400) + 0.5) / 400)
    square = 0.125 * (nodes + 1.0)
    r = np.sqrt(square)
    fit = np.polynomial.chebyshev.Chebyshev.fit
    cosine = fit(square, np.cos(2 * np.pi * r), 6, domain=[0, 0.25])
    sine = fit(square, -np.sin(2 * np.pi * r) / r, 5, domain=[0, 0.25])
    convert = np.polynomial.polynomial.Polynomial
    return (
        [float(v) for v in cosine.convert(kind=convert, domain=[-1, 1]).coef],
        [float(v) for v in sine.convert(kind=convert, domain=[-1, 1]).coef],
    )


COS_TERMS, SIN_TERMS = turn_coefficients()


def turn(s):
    r = s - jnp.round(s)
    y = r * r
    cosine = jnp.full_like(y, COS_TERMS[-1])
    for term in COS_TERMS[-2::-1]:
        cosine = cosine * y + term
    sine = jnp.full_like(y, SIN_TERMS[-1])
    for term in SIN_TERMS[-2::-1]:
        sine = sine * y + term
    return cosine, sine * r


def rounded(value):
    return value.astype(jnp.bfloat16)


def wide(value):
    return value.astype(jnp.float32)


class Copies:
    def __init__(self, send_sems, recv_sems):
        self.send_sems, self.recv_sems = send_sems, recv_sems
        self.all = []

    def start(self, source, target, device):
        place = len(self.all)
        copy = pltpu.make_async_remote_copy(
            src_ref=source,
            dst_ref=target,
            send_sem=self.send_sems.at[place],
            recv_sem=self.recv_sems.at[place],
            device_id=device,
            device_id_type=MESH,
        )
        copy.start()
        self.all.append(copy)
        return copy

    def finish(self):
        for copy in self.all:
            copy.wait_send()


class Ring:
    def __init__(self, copies, me, left, right, source, first, second, near, far):
        self.copies, self.left, self.right = copies, left, right
        self.across = source(lax.rem(me + 2, RING))
        self.after = source(lax.rem(me + 1, RING))
        self.before = source(lax.rem(me + 3, RING))
        self.own = source(me)
        self.first, self.second, self.near, self.far = first, second, near, far

    def step_1(self):
        self.from_left = self.copies.start(self.across.at[self.first], self.near.at[0], self.right)
        self.from_right = self.copies.start(self.across.at[self.second], self.near.at[1], self.left)

    def step_2(self):
        self.from_left.wait_recv()
        half = self.after.at[self.first]
        half[...] = rounded(wide(half[...]) + wide(self.near[0]))
        from_left = self.copies.start(self.after, self.far.at[0], self.right)
        self.from_right.wait_recv()
        half = self.before.at[self.second]
        half[...] = rounded(wide(half[...]) + wide(self.near[1]))
        from_right = self.copies.start(self.before, self.far.at[1], self.left)
        self.from_left, self.from_right = from_left, from_right

    def total(self):
        self.from_left.wait_recv()
        self.from_right.wait_recv()
        return wide(self.own[...]) + wide(self.far[0]) + wide(self.far[1])


PAIRS = [(0, 0, 0), (1, 0, 0), (0, 0, 1), (0, 1, 0), (0, 1, 1), (1, 0, 1), (1, 1, 0), (1, 1, 1)]
PARTS = [(0, 2), (2, 5), (5, 8)]
UPWARD = [[(0, 1), (1, 2)], [(2, 5)], [(5, 8)]]
N_COPIES = 4 + 4 * 4 + 4 * 4 + 2 * 3 + 2 * 8 + 3 * 3 + 4


def slab_matrix():
    place = lax.broadcasted_iota(jnp.int32, (LANES, LANES), 0)
    function = lax.broadcasted_iota(jnp.int32, (LANES, LANES), 1)
    x, z, i = place // 64, (place // 16) % RING, place % 16
    held = jnp.where(i < SLAB, SLAB * (z * RING + x) + i, -1)
    return jnp.where(held == function, 1.0, 0.0).astype(jnp.bfloat16)


def kernel(
    coeffs_hbm, offsets_hbm, moments_hbm, centers_hbm, flags_hbm, weights_hbm, boost_hbm,
    pieces_hbm, headings_hbm, places_hbm,
    lower_ref, upper_ref,
    coeffs_ref, offsets_ref, moments_ref, centers_ref, flags_ref, weights_ref, boost_ref,
    pieces_ref, headings_ref, places_ref,
    slabs, geometry, coeffs_pad, turned, samples, part, x_near, x_far, z_send, z_near, z_far,
    patterns, plain, turned_send, turned_recv, lobe_pair, lobe_all,
    zp, z_recv, up_send, up_recv,
    send_sems, recv_sems, load_sems,
):
    group = lax.axis_index("grp")
    groups = lax.axis_size("grp")
    sub = lax.axis_index("sub")
    x, z = lax.rem(sub, RING), sub // RING
    z_odd = lax.rem(z, 2)

    def at(z_to, x_to):
        return {"sub": z_to * RING + x_to}

    def along(me, steps):
        return lax.rem(me + steps, RING)

    x_peers = [at(z, along(x, d)) for d in range(1, RING)]
    z_peers = [at(along(z, d), x) for d in range(1, RING)]
    z_pair = at(z + 1 - 2 * z_odd, x)

    def other(shift, d=0):
        return {"grp": lax.rem(group + shift + groups, groups), "sub": z * RING + along(x, d)}

    plain[:, :, :, ROWS:] = jnp.zeros((2, RING, 2, HOLD - ROWS, LANES), jnp.bfloat16)

    barrier = pltpu.get_barrier_semaphore()
    group_peers = [other(shift, d) for shift in (1, -1, 2, -2) for d in range(RING)]
    peers = x_peers + z_peers + group_peers
    for peer in peers:
        pl.semaphore_signal(barrier, inc=1, device_id=peer, device_id_type=MESH)

    loads = [
        pltpu.make_async_copy(source, target, load_sems.at[k])
        for k, (source, target) in enumerate(
            [
                (offsets_hbm, offsets_ref),
                (moments_hbm, moments_ref),
                (pieces_hbm, pieces_ref),
                (coeffs_hbm, coeffs_ref),
                (weights_hbm, weights_ref),
                (boost_hbm, boost_ref),
                (centers_hbm, centers_ref),
                (flags_hbm, flags_ref),
                (headings_hbm, headings_ref),
                (places_hbm, places_ref),
            ]
        )
    ]
    for load in loads:
        load.start()

    copies = Copies(send_sems, recv_sems)
    slabs[...] = slab_matrix()
    for load in loads[:4]:
        load.wait()

    for block in range(2):
        geometry[block] = jnp.zeros((DEPTH, geometry.shape[2]), jnp.float32)
        for axis in range(3):
            offset = wide(offsets_ref[axis])[block : block + 1]
            moment = wide(moments_ref[axis])[block : block + 1]
            for piece in range(3):
                geometry[block, 3 * piece + axis : 3 * piece + axis + 1, :] = offset
                geometry[block, 9 + 3 * piece + axis : 10 + 3 * piece + axis, :] = moment
        coeffs_pad[block] = rounded(
            jnp.dot(slabs[:, :BASIS], coeffs_ref[block], preferred_element_type=jnp.float32)
        )

    def project(owner, block):
        turned[...] = jnp.dot(
            pieces_ref[owner], rounded(geometry[block]), preferred_element_type=jnp.float32
        )

        def rows_of(step, carried):
            low = pl.multiple_of(step * 16, 16)
            half, inner = step // 3, pl.multiple_of(lax.rem(step, 3) * 16, 16)
            cosine, sine = turn(turned[pl.ds(low, 16), :])
            for polar in range(2):
                weight = turned[pl.ds(low + (polar + 1) * 2 * ROWS, 16), :]
                samples[0, polar * 2 + half, pl.ds(inner, 16), :] = rounded(weight * cosine)
                samples[1, polar * 2 + half, pl.ds(inner, 16), :] = rounded(weight * sine)
            return carried

        lax.fori_loop(0, 6, rows_of, 0)
        sums = lax.dot_general(
            samples[...].reshape(8 * ROWS, samples.shape[3]),
            coeffs_pad[block],
            (((1,), (1,)), ((), ())),
            preferred_element_type=jnp.float32,
        )
        for side in range(2):
            part[owner, block, :, :, side] = rounded(sums[:, side * 128 : side * 128 + 128]).reshape(
                2, RING, ROWS, 128
            )

    across, after, before = along(x, 2), along(x, 1), along(x, 3)
    steps = [(b, c) for b in range(2) for c in range(2)]
    x_rings = [
        Ring(
            copies, x, x_peers[2], x_peers[0], lambda o, b=b, c=c: part.at[o, b, c],
            pl.ds(0, 2), pl.ds(2, 2), x_near.at[k], x_far.at[k],
        )
        for k, (b, c) in enumerate(steps)
    ]
    z_rings = [
        Ring(
            copies, z, z_peers[2], z_peers[0], lambda o, k=k: z_send.at[k, o],
            0, 1, z_near.at[k], z_far.at[k],
        )
        for k in range(4)
    ]

    def cross(k):
        z_send[k] = rounded(x_rings[k].total())
        z_rings[k].step_1()

    def keep(k):
        total = z_rings[k].total()
        for side in range(2):
            patterns[k // 2, k % 2, 0:ROWS, side * 128 : side * 128 + 128] = total[side]

    project(across, 0)
    pl.semaphore_wait(barrier, len(peers))
    x_rings[0].step_1()
    x_rings[1].step_1()
    project(across, 1)
    x_rings[2].step_1()
    x_rings[3].step_1()

    loads[4].wait()
    loads[5].wait()
    lobe_pair[0] = jnp.zeros((8, 128), jnp.float32)
    lobe_pair[0, 0:1, 0 : weights_ref.shape[1]] = weights_ref[...]
    lobe_pair[0, 1:2, 0 : weights_ref.shape[1]] = boost_ref[...]
    paired = copies.start(lobe_pair.at[0], lobe_pair.at[1], z_pair)

    project(after, 0)
    project(before, 0)
    x_rings[0].step_2()
    x_rings[1].step_2()
    project(after, 1)
    project(before, 1)
    x_rings[2].step_2()
    x_rings[3].step_2()
    project(x, 0)
    project(x, 1)
    paired.wait_recv()
    lobe_all[0] = lobe_pair[...]
    lobes = [copies.start(lobe_all.at[0], lobe_all.at[d], x_peers[d - 1]) for d in range(1, RING)]
    patterns[...] = jnp.zeros_like(patterns)
    cross(0)
    cross(1)
    z_rings[0].step_2()
    cross(2)
    z_rings[1].step_2()
    cross(3)
    z_rings[2].step_2()

    gathered = {}

    def settle(block):
        pattern = rounded(patterns[block])
        turned_send[block] = rounded(jnp.transpose(wide(pattern).reshape(2 * HOLD, LANES))).reshape(
            RING, HOLD, 2 * HOLD
        )
        for r in range(ROUND_TOTAL):
            for d in range(RING):
                gathered[block, r, d] = copies.start(
                    turned_send.at[block, along(x, d)], turned_recv.at[r, block, d], other(r + 1, d)
                )
        rows = pl.ds(0, ROWS)
        plain[block, 0, :, rows] = rounded(
            jnp.dot(pattern.reshape(2 * HOLD, LANES), slabs[...], preferred_element_type=jnp.float32)
        ).reshape(2, HOLD, LANES)[:, :ROWS]
        for d in range(1, RING):
            gathered[block, d] = copies.start(
                plain.at[block, 0, :, rows], plain.at[block, d, :, rows], x_peers[d - 1]
            )

    keep(0)
    keep(1)
    settle(0)
    z_rings[3].step_2()

    for load in loads[6:]:
        load.wait()
    row = lax.broadcasted_iota(jnp.int32, (8, 128), 0)
    flag_column = jnp.zeros((8, 128), jnp.float32)
    gaps = [jnp.zeros((8, 128), jnp.float32) for _ in range(3)]
    for k, (r, i, j) in enumerate(PAIRS):
        m = group * 2 + i
        n = lax.rem(group - r - 1 + groups, groups) * 2 + j
        flag_column = jnp.where(row == k, flags_ref[m, n].astype(jnp.float32), flag_column)
        for axis in range(3):
            gap = centers_ref[axis, m] - centers_ref[axis, n]
            gaps[axis] = jnp.where(row == k, gap, gaps[axis])
    odd = z_odd.astype(jnp.float32)
    below = lax.broadcasted_iota(jnp.int32, (128, 128), 0)
    sign = jnp.where(lax.broadcasted_iota(jnp.int32, (8, 128), 1) < HOLD, 1.0, -1.0)
    for lobe in lobes:
        lobe.wait_recv()
    cosines, sines = [], []
    for d in range(RING):
        source = lax.rem(x - d + RING, RING)
        facing = lax.rem(2 * x - d - 3 + 2 * RING, RING)
        table = source * 2 + z_odd
        near = lobe_all[d, 0] * (1.0 - odd) + lobe_all[d, 1] * odd
        far = lobe_all[facing, 1] * (1.0 - odd) + lobe_all[facing, 0] * odd
        place = places_ref[table]
        sums = jnp.dot(
            near, jnp.where(below == place[0:1], 1.0, 0.0),
            precision=lax.Precision.HIGHEST, preferred_element_type=jnp.float32,
        ) + jnp.dot(
            far, jnp.where(below == place[1:2], 1.0, 0.0),
            precision=lax.Precision.HIGHEST, preferred_element_type=jnp.float32,
        )
        heading = headings_ref[table]
        cosine, sine = turn(heading[0:1] * gaps[0] + heading[1:2] * gaps[1] + heading[2:3] * gaps[2])
        amplitude = (sums[0:1] + flag_column * sums[1:2]) * (1.0 / math.sqrt(LOBE_TOTAL))
        cosines.append(amplitude * cosine)
        sines.append(amplitude * sine * sign)

    def couple(k):
        r, i, j = PAIRS[k]
        carries = []
        for d in range(RING):
            right = wide(turned_recv[r, j, d])
            carries.append(
                rounded(
                    cosines[d][k : k + 1] * right + sines[d][k : k + 1] * pltpu.roll(right, HOLD, 1)
                )
            )
        total = jnp.dot(
            jnp.concatenate(carries, axis=1),
            plain[i].reshape(RING * 2 * HOLD, LANES),
            preferred_element_type=jnp.float32,
        )
        zp[:, k] = rounded(total).reshape(RING, 16, LANES)

    def arrived(block, rounds):
        for r in rounds:
            for d in range(RING):
                gathered[block, r, d].wait_recv()

    def arrived_own(block):
        for d in range(1, RING):
            gathered[block, d].wait_recv()

    spread = []

    def scatter(p):
        low, high = PARTS[p]
        for k in range(low, high):
            couple(k)
        pairs = pl.ds(low, high - low)
        spread.append(
            [
                copies.start(zp.at[along(z, d), pairs], z_recv.at[d - 1, pairs], z_peers[d - 1])
                for d in range(1, RING)
            ]
        )

    arrived(0, [0, 1])
    arrived_own(0)
    scatter(0)
    keep(2)
    keep(3)
    settle(1)
    arrived(1, [0])
    arrived_own(1)
    scatter(1)
    arrived(1, [1])
    scatter(2)

    back = []
    for p, (low, high) in enumerate(PARTS):
        for copy in spread[p]:
            copy.wait_recv()
        pairs = pl.ds(low, high - low)
        total = wide(zp[z, pairs])
        for d in range(1, RING):
            total = total + wide(z_recv[d - 1, pairs])
        up_send[pairs] = rounded(total)
        for first, last in UPWARD[p]:
            mine = pl.ds(first, last - first)
            back.append(copies.start(up_send.at[mine], up_recv.at[mine], other(-PAIRS[first][0] - 1)))
        for k in range(low, high):
            r, i, j = PAIRS[k]
            lower_ref[i, r, :, j, :] = total[k - low, :SLAB, :BASIS]
    for copy in back:
        copy.wait_recv()
    for k, (r, i, j) in enumerate(PAIRS):
        upper_ref[j, r, :, i, :] = wide(up_recv[k])[:SLAB, :BASIS]
    copies.finish()


def shards(coeffs, offsets, moments, centers, near_flags, lobe_weights, near_boost):
    pieces, headings, places = grid_tables()
    unknowns = coeffs.shape[2]
    bf16, f32 = jnp.bfloat16, jnp.float32
    operands = (
        coeffs,
        jnp.transpose(offsets, (1, 0, 2)),
        jnp.transpose(moments, (1, 0, 2)),
        jnp.transpose(centers),
        near_flags,
        lobe_weights.reshape(1, -1),
        near_boost.reshape(1, -1),
        jnp.asarray(pieces),
        jnp.asarray(headings),
        jnp.asarray(places),
    )
    held = [pltpu.SMEM if k in (3, 4) else pltpu.VMEM for k in range(len(operands))]
    vmem = pl.BlockSpec(memory_space=pltpu.VMEM)
    out = jax.ShapeDtypeStruct((2, ROUND_TOTAL, SLAB, 2, BASIS), f32)
    lower, upper = pl.pallas_call(
        kernel,
        out_shape=(out, out),
        in_specs=[pl.BlockSpec(memory_space=pltpu.HBM)] * len(operands),
        out_specs=(vmem, vmem),
        scratch_shapes=[
            *(space(operand.shape, operand.dtype) for space, operand in zip(held, operands)),
            pltpu.VMEM((LANES, LANES), bf16),
            pltpu.VMEM((2, DEPTH, unknowns), f32),
            pltpu.VMEM((2, LANES, unknowns), bf16),
            pltpu.VMEM((6 * ROWS, unknowns), f32),
            pltpu.VMEM((2, RING, ROWS, unknowns), bf16),
            pltpu.VMEM((RING, 2, 2, RING, 2, ROWS, 128), bf16),
            pltpu.VMEM((4, 2, 2, 2, ROWS, 128), bf16),
            pltpu.VMEM((4, 2, RING, 2, ROWS, 128), bf16),
            pltpu.VMEM((4, RING, 2, ROWS, 128), bf16),
            pltpu.VMEM((4, 2, ROWS, 128), bf16),
            pltpu.VMEM((4, 2, 2, ROWS, 128), bf16),
            pltpu.VMEM((2, 2, HOLD, LANES), f32),
            pltpu.VMEM((2, RING, 2, HOLD, LANES), bf16),
            pltpu.VMEM((2, RING, HOLD, 2 * HOLD), bf16),
            pltpu.VMEM((ROUND_TOTAL, 2, RING, HOLD, 2 * HOLD), bf16),
            pltpu.VMEM((2, 8, 128), f32),
            pltpu.VMEM((RING, 2, 8, 128), f32),
            pltpu.VMEM((RING, 8, 16, LANES), bf16),
            pltpu.VMEM((RING - 1, 8, 16, LANES), bf16),
            pltpu.VMEM((8, 16, LANES), bf16),
            pltpu.VMEM((8, 16, LANES), bf16),
            pltpu.SemaphoreType.DMA((N_COPIES,)),
            pltpu.SemaphoreType.DMA((N_COPIES,)),
            pltpu.SemaphoreType.DMA((len(operands),)),
        ],
        compiler_params=pltpu.CompilerParams(
            collective_id=0, has_side_effects=True, vmem_limit_bytes=62 * 1024 * 1024
        ),
        name="fill",
    )(*operands)
    return jnp.transpose(lower, (0, 1, 3, 4, 2)), jnp.transpose(upper, (0, 1, 3, 2, 4))


def solution(mesh):
    placed = (
        P("grp", None, "sub"),
        P("grp", None, "sub"),
        P("grp", None, "sub"),
        P(),
        P(),
        P("sub"),
        P("sub"),
    )
    return jax.shard_map(
        shards,
        mesh=mesh,
        in_specs=placed,
        out_specs=(P("grp", None, None, None, "sub"), P("grp", None, None, "sub", None)),
        check_vma=False,
    )
```

```python
import math

import jax
import jax.numpy as jnp
import numpy as np
from jax import lax
from jax.experimental import pallas as pl
from jax.experimental.pallas import tpu as pltpu
from jax.sharding import PartitionSpec as P

THETAS = 20
PHIS = 36
DIRS = 720
LOBE_TOTAL = 1440
ROUND_TOTAL = 2
BASIS = 240
RING = 4
HALF = 45
ROWS = 48
HOLD = 64
SLAB = 15
LANES = 256
DEPTH = 32
MESH = pl.DeviceIdType.MESH
ZDIRECT = True
ORDER = 2
VMEM_MB = 48


def heading_of(t):
    theta = np.pi * ((t // PHIS) + 0.5) / THETAS
    azimuth = 2.0 * np.pi * (t % PHIS) / PHIS
    st, ct, sa, ca = np.sin(theta), np.cos(theta), np.sin(azimuth), np.cos(azimuth)
    heading = np.stack([st * ca, st * sa, ct], axis=-1)
    along_theta = np.stack([ct * ca, ct * sa, -st], axis=-1)
    along_phi = np.stack([-sa, ca, np.zeros_like(sa)], axis=-1)
    return heading, along_theta, along_phi


def split3(value):
    value = value.astype(np.float32)
    parts = []
    for _ in range(3):
        part = value.astype(jnp.bfloat16)
        parts.append(part)
        value = value - part.astype(np.float32)
    return np.concatenate(parts, axis=-1)


def grid_tables():
    pieces = np.zeros((RING, 3, 2, ROWS, DEPTH), jnp.bfloat16)
    headings = np.zeros((2 * RING, 8, 2, HOLD), np.float32)
    places = np.full((2 * RING, 8, 2, HOLD), -1, np.int32)
    for xo in range(RING):
        for dh in range(2):
            t = 90 * xo + HALF * dh + np.arange(HALF)
            heading, along_theta, along_phi = heading_of(t)
            pieces[xo, 0, dh, :HALF, 0:9] = split3(0.5 * heading)
            pieces[xo, 1, dh, :HALF, 9:18] = split3(along_theta)
            pieces[xo, 2, dh, :HALF, 9:18] = split3(along_phi)
            headings[2 * xo + dh, 0:3, :, :HALF] = 0.5 * heading.T[:, None]
            opposite = PHIS * (THETAS - 1 - t // PHIS) + (t % PHIS + PHIS // 2) % PHIS - 90 * (7 - xo)
            assert opposite.min() >= 0 and opposite.max() < 90
            places[2 * xo + dh, 0, :, :HALF] = t - 90 * xo
            places[2 * xo + dh, 1, :, :HALF] = opposite
    wide_as = (2 * RING, 8, 2 * HOLD)
    return pieces.reshape(RING, 6 * ROWS, DEPTH), headings.reshape(wide_as), places.reshape(wide_as)


def turn_coefficients():
    nodes = np.cos(np.pi * (np.arange(400) + 0.5) / 400)
    square = 0.125 * (nodes + 1.0)
    r = np.sqrt(square)
    fit = np.polynomial.chebyshev.Chebyshev.fit
    cosine = fit(square, np.cos(2 * np.pi * r), 6, domain=[0, 0.25])
    sine = fit(square, -np.sin(2 * np.pi * r) / r, 5, domain=[0, 0.25])
    convert = np.polynomial.polynomial.Polynomial
    return (
        [float(v) for v in cosine.convert(kind=convert, domain=[-1, 1]).coef],
        [float(v) for v in sine.convert(kind=convert, domain=[-1, 1]).coef],
    )


COS_TERMS, SIN_TERMS = turn_coefficients()


def turn(s):
    r = s - jnp.round(s)
    y = r * r
    cosine = jnp.full_like(y, COS_TERMS[-1])
    for term in COS_TERMS[-2::-1]:
        cosine = cosine * y + term
    sine = jnp.full_like(y, SIN_TERMS[-1])
    for term in SIN_TERMS[-2::-1]:
        sine = sine * y + term
    return cosine, sine * r


def rounded(value):
    return value.astype(jnp.bfloat16)


def wide(value):
    return value.astype(jnp.float32)


class Copies:
    def __init__(self, send_sems, recv_sems):
        self.send_sems, self.recv_sems = send_sems, recv_sems
        self.all = []

    def start(self, source, target, device, arrival=None):
        place = len(self.all)
        copy = pltpu.make_async_remote_copy(
            src_ref=source,
            dst_ref=target,
            send_sem=self.send_sems.at[place],
            recv_sem=self.recv_sems.at[place] if arrival is None else arrival,
            device_id=device,
            device_id_type=MESH,
        )
        copy.start()
        self.all.append(copy)
        return copy

    def arrive(self, target, arrival, device):
        pltpu.make_async_remote_copy(
            src_ref=target,
            dst_ref=target,
            send_sem=self.send_sems.at[0],
            recv_sem=arrival,
            device_id=device,
            device_id_type=MESH,
        ).wait_recv()

    def finish(self):
        for copy in self.all:
            copy.wait_send()


class Ring:
    def __init__(self, copies, me, left, right, source, first, second, near, far):
        self.copies, self.left, self.right = copies, left, right
        self.across = source(lax.rem(me + 2, RING))
        self.after = source(lax.rem(me + 1, RING))
        self.before = source(lax.rem(me + 3, RING))
        self.own = source(me)
        self.first, self.second, self.near, self.far = first, second, near, far

    def step_1(self):
        self.from_left = self.copies.start(self.across.at[self.first], self.near.at[0], self.right)
        self.from_right = self.copies.start(self.across.at[self.second], self.near.at[1], self.left)

    def step_2(self):
        self.from_left.wait_recv()
        half = self.after.at[self.first]
        half[...] = rounded(wide(half[...]) + wide(self.near[0]))
        from_left = self.copies.start(self.after, self.far.at[0], self.right)
        self.from_right.wait_recv()
        half = self.before.at[self.second]
        half[...] = rounded(wide(half[...]) + wide(self.near[1]))
        from_right = self.copies.start(self.before, self.far.at[1], self.left)
        self.from_left, self.from_right = from_left, from_right

    def total(self):
        self.from_left.wait_recv()
        self.from_right.wait_recv()
        return wide(self.own[...]) + wide(self.far[0]) + wide(self.far[1])


PAIRS = [(0, 0, 0), (1, 0, 0), (0, 0, 1), (0, 1, 0), (0, 1, 1), (1, 0, 1), (1, 1, 0), (1, 1, 1)]
PARTS = [(0, 2), (2, 5), (5, 8)]
UPWARD = [[(0, 1), (1, 2)], [(2, 5)], [(5, 8)]]
N_COPIES = 4 + 4 * 4 + 4 * 4 + 4 * 3 + 4 * 4 + 3 * 3 + 4


def slab_matrix():
    place = lax.broadcasted_iota(jnp.int32, (LANES, LANES), 0)
    function = lax.broadcasted_iota(jnp.int32, (LANES, LANES), 1)
    x, z, i = place // 64, (place // 16) % RING, place % 16
    held = jnp.where(i < SLAB, SLAB * (z * RING + x) + i, -1)
    return jnp.where(held == function, 1.0, 0.0).astype(jnp.bfloat16)


def kernel(
    coeffs_hbm, offsets_hbm, moments_hbm, centers_hbm, flags_hbm, weights_hbm, boost_hbm,
    pieces_hbm, headings_hbm, places_hbm,
    lower_ref, upper_ref,
    coeffs_ref, offsets_ref, moments_ref, centers_ref, flags_ref, weights_ref, boost_ref,
    pieces_ref, headings_ref, places_ref,
    slabs, geometry, coeffs_pad, turned, samples, part, x_near, x_far, z_send, z_near, z_far,
    left, turned_send, right, lobe_pair, lobe_all,
    zp, z_recv, up_send, up_recv,
    send_sems, recv_sems, left_sems, right_sems, lobe_sems, load_sems,
):
    group = lax.axis_index("grp")
    groups = lax.axis_size("grp")
    sub = lax.axis_index("sub")
    x, z = lax.rem(sub, RING), sub // RING
    z_odd = lax.rem(z, 2)

    def at(z_to, x_to):
        return {"sub": z_to * RING + x_to}

    def along(me, steps):
        return lax.rem(me + steps, RING)

    x_peers = [at(z, along(x, d)) for d in range(1, RING)]
    z_peers = [at(along(z, d), x) for d in range(1, RING)]
    z_pair = at(z + 1 - 2 * z_odd, x)

    def other(shift, x_to):
        return {"grp": lax.rem(group + shift + groups, groups), "sub": z * RING + x_to}

    left[:, :, :, :, ROWS:] = jnp.zeros((2, 2, RING, 2, HOLD - ROWS, 128), jnp.bfloat16)

    barrier = pltpu.get_barrier_semaphore()
    group_peers = [other(shift, x_to) for shift in (1, -1, 2, -2) for x_to in range(RING)]
    peers = x_peers + z_peers + group_peers
    for peer in peers:
        pl.semaphore_signal(barrier, inc=1, device_id=peer, device_id_type=MESH)

    loads = [
        pltpu.make_async_copy(source, target, load_sems.at[k])
        for k, (source, target) in enumerate(
            [
                (offsets_hbm, offsets_ref),
                (moments_hbm, moments_ref),
                (pieces_hbm, pieces_ref),
                (coeffs_hbm, coeffs_ref),
                (weights_hbm, weights_ref),
                (boost_hbm, boost_ref),
                (centers_hbm, centers_ref),
                (flags_hbm, flags_ref),
                (headings_hbm, headings_ref),
                (places_hbm, places_ref),
            ]
        )
    ]
    for load in loads:
        load.start()

    copies = Copies(send_sems, recv_sems)
    slabs[...] = slab_matrix()
    for load in loads[:4]:
        load.wait()

    def prepare(block):
        geometry[block] = jnp.zeros((DEPTH, geometry.shape[2]), jnp.float32)
        for axis in range(3):
            offset = wide(offsets_ref[axis])[block : block + 1]
            moment = wide(moments_ref[axis])[block : block + 1]
            for piece in range(3):
                geometry[block, 3 * piece + axis : 3 * piece + axis + 1, :] = offset
                geometry[block, 9 + 3 * piece + axis : 10 + 3 * piece + axis, :] = moment
        coeffs_pad[block] = rounded(
            jnp.dot(slabs[:, :BASIS], coeffs_ref[block], preferred_element_type=jnp.float32)
        )

    def project(owner, block):
        turned[...] = jnp.dot(
            pieces_ref[owner], rounded(geometry[block]), preferred_element_type=jnp.float32
        )

        def rows_of(step, carried):
            low = pl.multiple_of(step * 16, 16)
            half, inner = step // 3, pl.multiple_of(lax.rem(step, 3) * 16, 16)
            cosine, sine = turn(turned[pl.ds(low, 16), :])
            for polar in range(2):
                weight = turned[pl.ds(low + (polar + 1) * 2 * ROWS, 16), :]
                samples[polar * 2 + half, 0, pl.ds(inner, 16), :] = rounded(weight * cosine)
                samples[polar * 2 + half, 1, pl.ds(inner, 16), :] = rounded(weight * sine)
            return carried

        lax.fori_loop(0, 6, rows_of, 0)
        sums = lax.dot_general(
            samples[...].reshape(8 * ROWS, samples.shape[3]),
            coeffs_pad[block],
            (((1,), (1,)), ((), ())),
            preferred_element_type=jnp.float32,
        )
        for side in range(2):
            part[owner, block, side] = rounded(sums[:, side * 128 : side * 128 + 128]).reshape(
                RING, 2, ROWS, 128
            )

    across, after, before = along(x, 2), along(x, 1), along(x, 3)
    steps = [(block, side) for block in range(2) for side in range(2)]
    x_rings = [
        Ring(
            copies, x, x_peers[2], x_peers[0], lambda o, b=b, side=side: part.at[o, b, side],
            pl.ds(0, 2), pl.ds(2, 2), x_near.at[k], x_far.at[k],
        )
        for k, (b, side) in enumerate(steps)
    ]
    z_rings = [
        Ring(
            copies, z, z_peers[2], z_peers[0], lambda o, k=k: z_send.at[k, o],
            0, 1, z_near.at[k], z_far.at[k],
        )
        for k in range(4)
    ]
    z_direct = {}

    def cross(k):
        z_send[k] = rounded(x_rings[k].total())
        if ZDIRECT:
            z_direct[k] = [
                copies.start(z_send.at[k, along(z, d)], z_far.at[k, d - 1], z_peers[d - 1])
                for d in (2, 1, 3)
            ]
        else:
            z_rings[k].step_1()

    def z_step_2(k):
        if not ZDIRECT:
            z_rings[k].step_2()

    def settle(k):
        block, side = steps[k]
        if ZDIRECT:
            for copy in z_direct[k]:
                copy.wait_recv()
            total = wide(z_send[k, z])
            for d in range(1, RING):
                total = total + wide(z_far[k, d - 1])
        else:
            total = z_rings[k].total()
        pattern = rounded(total)
        mine = left.at[side, block, x, :, pl.ds(0, ROWS)]
        mine[...] = pattern
        for d in range(1, RING):
            copies.start(mine, mine, x_peers[d - 1], left_sems.at[side, block, x])
        held = jnp.concatenate([wide(pattern), jnp.zeros((2, HOLD - ROWS, 128), jnp.float32)], axis=1)
        turned_send[k] = rounded(jnp.transpose(held.reshape(2 * HOLD, 128))).reshape(2, HOLD, 2 * HOLD)
        for r in range(ROUND_TOTAL):
            for e in range(2):
                copies.start(
                    turned_send.at[k, e],
                    right.at[r, block, x],
                    other(r + 1, 2 * side + e),
                    right_sems.at[r, block, x],
                )

    prepare(0)
    project(across, 0)
    pl.semaphore_wait(barrier, len(peers))
    x_rings[0].step_1()
    x_rings[1].step_1()
    prepare(1)
    project(across, 1)
    x_rings[2].step_1()
    x_rings[3].step_1()

    loads[4].wait()
    loads[5].wait()
    lobe_pair[0] = jnp.zeros((8, 128), jnp.float32)
    lobe_pair[0, 0:1, 0 : weights_ref.shape[1]] = weights_ref[...]
    lobe_pair[0, 1:2, 0 : weights_ref.shape[1]] = boost_ref[...]
    paired = copies.start(lobe_pair.at[0], lobe_pair.at[1], z_pair)

    project(after, 0)
    project(before, 0)
    x_rings[0].step_2()
    x_rings[1].step_2()
    project(after, 1)
    project(before, 1)
    x_rings[2].step_2()
    x_rings[3].step_2()
    project(x, 0)
    project(x, 1)
    cross(0)
    cross(1)
    z_step_2(0)
    cross(2)
    z_step_2(1)
    cross(3)
    paired.wait_recv()
    lobe_all[x] = lobe_pair[...]
    for d in range(1, RING):
        copies.start(lobe_all.at[x], lobe_all.at[x], x_peers[d - 1], lobe_sems.at[x])
    z_step_2(2)
    settle(0)
    z_step_2(3)
    settle(1)

    for load in loads[6:]:
        load.wait()
    row = lax.broadcasted_iota(jnp.int32, (8, 128), 0)
    flag_column = jnp.zeros((8, 128), jnp.float32)
    gaps = [jnp.zeros((8, 128), jnp.float32) for _ in range(3)]
    for k, (r, i, j) in enumerate(PAIRS):
        m = group * 2 + i
        n = lax.rem(group - r - 1 + groups, groups) * 2 + j
        flag_column = jnp.where(row == k, flags_ref[m, n].astype(jnp.float32), flag_column)
        for axis in range(3):
            gap = centers_ref[axis, m] - centers_ref[axis, n]
            gaps[axis] = jnp.where(row == k, gap, gaps[axis])
    odd = z_odd.astype(jnp.float32)
    below = lax.broadcasted_iota(jnp.int32, (128, 128), 0)
    sign = jnp.where(lax.broadcasted_iota(jnp.int32, (8, 128), 1) < HOLD, 1.0, -1.0)
    for d in range(1, RING):
        there = along(x, d)
        copies.arrive(lobe_all.at[there], lobe_sems.at[there], x_peers[d - 1])
    cosines, sines = [], []
    for source in range(RING):
        near = lobe_all[source, 0] * (1.0 - odd) + lobe_all[source, 1] * odd
        far = lobe_all[3 - source, 1] * (1.0 - odd) + lobe_all[3 - source, 0] * odd
        table = source * 2 + z_odd
        place = places_ref[table]
        sums = jnp.dot(
            near, jnp.where(below == place[0:1], 1.0, 0.0),
            precision=lax.Precision.HIGHEST, preferred_element_type=jnp.float32,
        ) + jnp.dot(
            far, jnp.where(below == place[1:2], 1.0, 0.0),
            precision=lax.Precision.HIGHEST, preferred_element_type=jnp.float32,
        )
        heading = headings_ref[table]
        cosine, sine = turn(heading[0:1] * gaps[0] + heading[1:2] * gaps[1] + heading[2:3] * gaps[2])
        amplitude = (sums[0:1] + flag_column * sums[1:2]) * (1.0 / math.sqrt(LOBE_TOTAL))
        cosines.append(amplitude * cosine)
        sines.append(amplitude * sine * sign)

    def couple(k):
        r, i, j = PAIRS[k]
        carries = []
        for source in range(RING):
            value = wide(right[r, j, source])
            carries.append(
                rounded(
                    cosines[source][k : k + 1] * value
                    + sines[source][k : k + 1] * pltpu.roll(value, HOLD, 1)
                )
            )
        carry = jnp.concatenate(carries, axis=1)
        total = jnp.concatenate(
            [
                jnp.dot(
                    carry, left[side, i].reshape(RING * 2 * HOLD, 128), preferred_element_type=jnp.float32
                )
                for side in range(2)
            ],
            axis=1,
        )
        total = jnp.dot(rounded(total), slabs[...], preferred_element_type=jnp.float32)
        zp[:, k] = rounded(total).reshape(RING, 16, LANES)

    def arrived_right(r, block):
        for source in range(RING):
            copies.arrive(right.at[r, block, source], right_sems.at[r, block, source], other(-r - 1, source))

    def arrived_left(block):
        for side in range(2):
            for d in range(1, RING):
                there = along(x, d)
                copies.arrive(
                    left.at[side, block, there, :, pl.ds(0, ROWS)],
                    left_sems.at[side, block, there],
                    x_peers[d - 1],
                )

    spread = []

    def scatter(p):
        low, high = PARTS[p]
        for k in range(low, high):
            couple(k)
        pairs = pl.ds(low, high - low)
        spread.append(
            [
                copies.start(zp.at[along(z, d), pairs], z_recv.at[d - 1, pairs], z_peers[d - 1])
                for d in range(1, RING)
            ]
        )

    def early():
        arrived_left(0)
        arrived_right(0, 0)
        arrived_right(1, 0)
        scatter(0)

    if ORDER == 0:
        early()
        settle(2)
        settle(3)
    elif ORDER == 1:
        settle(2)
        early()
        settle(3)
    else:
        settle(2)
        settle(3)
        early()
    arrived_left(1)
    arrived_right(0, 1)
    scatter(1)
    arrived_right(1, 1)
    scatter(2)

    back = []
    for p, (low, high) in enumerate(PARTS):
        for copy in spread[p]:
            copy.wait_recv()
        pairs = pl.ds(low, high - low)
        total = wide(zp[z, pairs])
        for d in range(1, RING):
            total = total + wide(z_recv[d - 1, pairs])
        up_send[pairs] = rounded(total)
        for first, last in UPWARD[p]:
            mine = pl.ds(first, last - first)
            back.append(copies.start(up_send.at[mine], up_recv.at[mine], other(-PAIRS[first][0] - 1, x)))
        for k in range(low, high):
            r, i, j = PAIRS[k]
            lower_ref[i, r, :, j, :] = total[k - low, :SLAB, :BASIS]
    for copy in back:
        copy.wait_recv()
    for k, (r, i, j) in enumerate(PAIRS):
        upper_ref[j, r, :, i, :] = wide(up_recv[k])[:SLAB, :BASIS]
    copies.finish()


def shards(coeffs, offsets, moments, centers, near_flags, lobe_weights, near_boost):
    pieces, headings, places = grid_tables()
    unknowns = coeffs.shape[2]
    bf16, f32 = jnp.bfloat16, jnp.float32
    operands = (
        coeffs,
        jnp.transpose(offsets, (1, 0, 2)),
        jnp.transpose(moments, (1, 0, 2)),
        jnp.transpose(centers),
        near_flags,
        lobe_weights.reshape(1, -1),
        near_boost.reshape(1, -1),
        jnp.asarray(pieces),
        jnp.asarray(headings),
        jnp.asarray(places),
    )
    held = [pltpu.SMEM if k in (3, 4) else pltpu.VMEM for k in range(len(operands))]
    vmem = pl.BlockSpec(memory_space=pltpu.VMEM)
    out = pltpu.VMEM((2, ROUND_TOTAL, SLAB, 2, BASIS), f32)
    lower, upper = pl.pallas_call(
        kernel,
        out_shape=(out, out),
        in_specs=[pl.BlockSpec(memory_space=pltpu.HBM)] * len(operands),
        out_specs=(vmem, vmem),
        scratch_shapes=[
            *(space(operand.shape, operand.dtype) for space, operand in zip(held, operands)),
            pltpu.VMEM((LANES, LANES), bf16),
            pltpu.VMEM((2, DEPTH, unknowns), f32),
            pltpu.VMEM((2, LANES, unknowns), bf16),
            pltpu.VMEM((6 * ROWS, unknowns), f32),
            pltpu.VMEM((RING, 2, ROWS, unknowns), bf16),
            pltpu.VMEM((RING, 2, 2, RING, 2, ROWS, 128), bf16),
            pltpu.VMEM((4, 2, 2, 2, ROWS, 128), bf16),
            pltpu.VMEM((4, 2, RING, 2, ROWS, 128), bf16),
            pltpu.VMEM((4, RING, 2, ROWS, 128), bf16),
            pltpu.VMEM((4, 2, ROWS, 128), bf16),
            pltpu.VMEM((4, RING - 1, 2, ROWS, 128), bf16),
            pltpu.VMEM((2, 2, RING, 2, HOLD, 128), bf16),
            pltpu.VMEM((4, 2, HOLD, 2 * HOLD), bf16),
            pltpu.VMEM((ROUND_TOTAL, 2, RING, HOLD, 2 * HOLD), bf16),
            pltpu.VMEM((2, 8, 128), f32),
            pltpu.VMEM((RING, 2, 8, 128), f32),
            pltpu.VMEM((RING, 8, 16, LANES), bf16),
            pltpu.VMEM((RING - 1, 8, 16, LANES), bf16),
            pltpu.VMEM((8, 16, LANES), bf16),
            pltpu.VMEM((8, 16, LANES), bf16),
            pltpu.SemaphoreType.DMA((N_COPIES,)),
            pltpu.SemaphoreType.DMA((N_COPIES,)),
            pltpu.SemaphoreType.DMA((2, 2, RING)),
            pltpu.SemaphoreType.DMA((ROUND_TOTAL, 2, RING)),
            pltpu.SemaphoreType.DMA((RING,)),
            pltpu.SemaphoreType.DMA((len(operands),)),
        ],
        compiler_params=pltpu.CompilerParams(
            collective_id=0, has_side_effects=True, vmem_limit_bytes=VMEM_MB * 1024 * 1024
        ),
        name="fill",
    )(*(pltpu.with_memory_space_constraint(operand, pltpu.HBM) for operand in operands))
    return jnp.transpose(lower, (0, 1, 3, 4, 2)), jnp.transpose(upper, (0, 1, 3, 2, 4))


def solution(mesh):
    placed = (
        P("grp", None, "sub"),
        P("grp", None, "sub"),
        P("grp", None, "sub"),
        P(),
        P(),
        P("sub"),
        P("sub"),
    )
    return jax.shard_map(
        shards,
        mesh=mesh,
        in_specs=placed,
        out_specs=(P("grp", None, None, None, "sub"), P("grp", None, None, "sub", None)),
        check_vma=False,
    )
```

```python
import math

import jax
import jax.numpy as jnp
import numpy as np
from jax import lax
from jax.experimental import pallas as pl
from jax.experimental.pallas import tpu as pltpu
from jax.sharding import PartitionSpec as P

THETAS = 20
PHIS = 36
DIRS = 720
LOBE_TOTAL = 1440
ROUND_TOTAL = 2
BASIS = 240
RING = 4
HALF = 45
ROWS = 48
HOLD = 64
SLAB = 15
LANES = 256
DEPTH = 32
MESH = pl.DeviceIdType.MESH
ZRING = True
PRIO = True
CENTER = 2


def heading_of(t):
    theta = np.pi * ((t // PHIS) + 0.5) / THETAS
    azimuth = 2.0 * np.pi * (t % PHIS) / PHIS
    st, ct, sa, ca = np.sin(theta), np.cos(theta), np.sin(azimuth), np.cos(azimuth)
    heading = np.stack([st * ca, st * sa, ct], axis=-1)
    along_theta = np.stack([ct * ca, ct * sa, -st], axis=-1)
    along_phi = np.stack([-sa, ca, np.zeros_like(sa)], axis=-1)
    return heading, along_theta, along_phi


def split3(value):
    value = value.astype(np.float32)
    parts = []
    for _ in range(3):
        part = value.astype(jnp.bfloat16)
        parts.append(part)
        value = value - part.astype(np.float32)
    return np.concatenate(parts, axis=-1)


def grid_tables():
    pieces = np.zeros((RING, 3, 2, ROWS, DEPTH), jnp.bfloat16)
    headings = np.zeros((2 * RING, 8, 2, HOLD), np.float32)
    places = np.full((2 * RING, 8, 2, HOLD), -1, np.int32)
    for xo in range(RING):
        for dh in range(2):
            t = 90 * xo + HALF * dh + np.arange(HALF)
            heading, along_theta, along_phi = heading_of(t)
            pieces[xo, 0, dh, :HALF, 0:9] = split3(0.5 * heading)
            pieces[xo, 1, dh, :HALF, 9:18] = split3(along_theta)
            pieces[xo, 2, dh, :HALF, 9:18] = split3(along_phi)
            headings[2 * xo + dh, 0:3, :, :HALF] = 0.5 * heading.T[:, None]
            opposite = PHIS * (THETAS - 1 - t // PHIS) + (t % PHIS + PHIS // 2) % PHIS - 90 * (7 - xo)
            assert opposite.min() >= 0 and opposite.max() < 90
            places[2 * xo + dh, 0, :, :HALF] = t - 90 * xo
            places[2 * xo + dh, 1, :, :HALF] = opposite
    wide_as = (2 * RING, 8, 2 * HOLD)
    return pieces.reshape(RING, 6 * ROWS, DEPTH), headings.reshape(wide_as), places.reshape(wide_as)


def turn_coefficients():
    nodes = np.cos(np.pi * (np.arange(400) + 0.5) / 400)
    square = 0.125 * (nodes + 1.0)
    r = np.sqrt(square)
    fit = np.polynomial.chebyshev.Chebyshev.fit
    cosine = fit(square, np.cos(2 * np.pi * r), 6, domain=[0, 0.25])
    sine = fit(square, -np.sin(2 * np.pi * r) / r, 5, domain=[0, 0.25])
    convert = np.polynomial.polynomial.Polynomial
    return (
        [float(v) for v in cosine.convert(kind=convert, domain=[-1, 1]).coef],
        [float(v) for v in sine.convert(kind=convert, domain=[-1, 1]).coef],
    )


COS_TERMS, SIN_TERMS = turn_coefficients()


def turn(s):
    r = s - jnp.round(s)
    y = r * r
    cosine = jnp.full_like(y, COS_TERMS[-1])
    for term in COS_TERMS[-2::-1]:
        cosine = cosine * y + term
    sine = jnp.full_like(y, SIN_TERMS[-1])
    for term in SIN_TERMS[-2::-1]:
        sine = sine * y + term
    return cosine, sine * r


def rounded(value):
    return value.astype(jnp.bfloat16)


def wide(value):
    return value.astype(jnp.float32)


class Copies:
    def __init__(self, send_sems, recv_sems):
        self.send_sems, self.recv_sems = send_sems, recv_sems
        self.all = []

    def start(self, source, target, device, arrival=None):
        place = len(self.all)
        copy = pltpu.make_async_remote_copy(
            src_ref=source,
            dst_ref=target,
            send_sem=self.send_sems.at[place],
            recv_sem=self.recv_sems.at[place] if arrival is None else arrival,
            device_id=device,
            device_id_type=MESH,
        )
        copy.start()
        self.all.append(copy)
        return copy

    def arrive(self, target, arrival, device):
        pltpu.make_async_remote_copy(
            src_ref=target,
            dst_ref=target,
            send_sem=self.send_sems.at[0],
            recv_sem=arrival,
            device_id=device,
            device_id_type=MESH,
        ).wait_recv()

    def finish(self):
        for copy in self.all:
            copy.wait_send()


class Ring:
    def __init__(self, copies, me, left, right, source, first, second, near, far):
        self.copies, self.left, self.right = copies, left, right
        self.across = source(lax.rem(me + 2, RING))
        self.after = source(lax.rem(me + 1, RING))
        self.before = source(lax.rem(me + 3, RING))
        self.own = source(me)
        self.first, self.second, self.near, self.far = first, second, near, far

    def step_1(self):
        self.from_left = self.copies.start(self.across.at[self.first], self.near.at[0], self.right)
        self.from_right = self.copies.start(self.across.at[self.second], self.near.at[1], self.left)

    def step_2(self):
        self.from_left.wait_recv()
        half = self.after.at[self.first]
        half[...] = rounded(wide(half[...]) + wide(self.near[0]))
        from_left = self.copies.start(self.after, self.far.at[0], self.right)
        self.from_right.wait_recv()
        half = self.before.at[self.second]
        half[...] = rounded(wide(half[...]) + wide(self.near[1]))
        from_right = self.copies.start(self.before, self.far.at[1], self.left)
        self.from_left, self.from_right = from_left, from_right

    def total(self):
        self.from_left.wait_recv()
        self.from_right.wait_recv()
        return wide(self.own[...]) + wide(self.far[0]) + wide(self.far[1])


PAIRS = [(0, 0, 0), (1, 0, 0), (0, 0, 1), (0, 1, 0), (0, 1, 1), (1, 0, 1), (1, 1, 0), (1, 1, 1)]
PARTS = [(0, 2), (2, 5), (5, 8)]
UPWARD = [[(0, 1), (1, 2)], [(2, 5)], [(5, 8)]]
N_COPIES = 4 + 4 * 4 + 4 * 4 + 4 * 3 + 4 * 4 + 3 * 3 + 4


def slab_matrix():
    place = lax.broadcasted_iota(jnp.int32, (LANES, LANES), 0)
    function = lax.broadcasted_iota(jnp.int32, (LANES, LANES), 1)
    x, z, i = place // 64, (place // 16) % RING, place % 16
    held = jnp.where(i < SLAB, SLAB * (z * RING + x) + i, -1)
    return jnp.where(held == function, 1.0, 0.0).astype(jnp.bfloat16)


def kernel(
    coeffs_hbm, offsets_hbm, moments_hbm, centers_hbm, flags_hbm, weights_hbm, boost_hbm,
    pieces_hbm, headings_hbm, places_hbm,
    lower_ref, upper_ref,
    coeffs_ref, offsets_ref, moments_ref, centers_ref, flags_ref, weights_ref, boost_ref,
    pieces_ref, headings_ref, places_ref,
    slabs, geometry, coeffs_pad, turned, samples, part, x_near, x_far, z_send, z_near, z_far,
    left, turned_send, right, lobe_pair, lobe_all,
    zp, z_recv, up_send, up_recv,
    send_sems, recv_sems, left_sems, right_sems, lobe_sems, z_sems, load_sems, z_in, larger_in, smaller_in,
):
    group = lax.axis_index("grp")
    groups = lax.axis_size("grp")
    sub = lax.axis_index("sub")
    x, z = lax.rem(sub, RING), sub // RING
    z_odd = lax.rem(z, 2)

    def at(z_to, x_to):
        return {"sub": z_to * RING + x_to}

    def along(me, steps):
        return lax.rem(me + steps, RING)

    x_peers = [at(z, along(x, d)) for d in range(1, RING)]
    z_peers = [at(along(z, d), x) for d in range(1, RING)]
    z_pair = at(z + 1 - 2 * z_odd, x)

    def other(shift, x_to):
        return {"grp": lax.rem(group + shift + groups, groups), "sub": z * RING + x_to}

    left[:, :, :, :, ROWS:] = jnp.zeros((2, 2, RING, 2, HOLD - ROWS, 128), jnp.bfloat16)

    barrier = pltpu.get_barrier_semaphore()

    shifts = [(1, lax.rem(group + 1, groups)), (2, lax.rem(group + 2, groups))]
    shifts += [(-1, lax.rem(group + groups - 1, groups)), (-2, lax.rem(group + groups - 2, groups))]
    for peer in x_peers:
        pl.semaphore_signal(barrier, inc=1, device_id=peer, device_id_type=MESH)

    @pl.when(z != CENTER)
    def _():
        pl.semaphore_signal(barrier, inc=1, device_id=at(CENTER, x), device_id_type=MESH)

    smaller = 0
    for shift, place in shifts:
        smaller = smaller + jnp.where(place < group, 1, 0)

        @pl.when(group < place)
        def _(shift=shift):
            pl.semaphore_signal(barrier, inc=1, device_id=other(shift, x), device_id_type=MESH)

    greetings = RING - 1 + smaller + jnp.where(z == CENTER, RING - 1, 0)

    def enter():
        pl.semaphore_wait(barrier, greetings)

        @pl.when(z == CENTER)
        def _():
            for peer in z_peers:
                pl.semaphore_signal(z_in, inc=1, device_id=peer, device_id_type=MESH)

        for shift, place in shifts:

            @pl.when(place < group)
            def _(shift=shift):
                pl.semaphore_signal(larger_in, inc=1, device_id=other(shift, x), device_id_type=MESH)

    def enter_z():
        @pl.when(z != CENTER)
        def _():
            pl.semaphore_wait(z_in, 1)

    def enter_larger():
        @pl.when(smaller < 4)
        def _():
            pl.semaphore_wait(larger_in, 4 - smaller)

        for shift, place in shifts:

            @pl.when(group < place)
            def _(shift=shift):
                pl.semaphore_signal(smaller_in, inc=1, device_id=other(shift, x), device_id_type=MESH)

    def enter_smaller():
        @pl.when(smaller > 0)
        def _():
            pl.semaphore_wait(smaller_in, smaller)

    loads = [
        pltpu.make_async_copy(source, target, load_sems.at[k])
        for k, (source, target) in enumerate(
            [
                (offsets_hbm, offsets_ref),
                (moments_hbm, moments_ref),
                (pieces_hbm, pieces_ref),
                (coeffs_hbm, coeffs_ref),
                (weights_hbm, weights_ref),
                (boost_hbm, boost_ref),
                (centers_hbm, centers_ref),
                (flags_hbm, flags_ref),
                (headings_hbm, headings_ref),
                (places_hbm, places_ref),
            ]
        )
    ]
    for load in loads:
        load.start()

    copies = Copies(send_sems, recv_sems)
    slabs[...] = slab_matrix()
    for load in loads[:4]:
        load.wait()

    def prepare(block):
        geometry[block] = jnp.zeros((DEPTH, geometry.shape[2]), jnp.float32)
        for axis in range(3):
            offset = wide(offsets_ref[axis])[block : block + 1]
            moment = wide(moments_ref[axis])[block : block + 1]
            for piece in range(3):
                geometry[block, 3 * piece + axis : 3 * piece + axis + 1, :] = offset
                geometry[block, 9 + 3 * piece + axis : 10 + 3 * piece + axis, :] = moment
        coeffs_pad[block] = rounded(
            jnp.dot(slabs[:, :BASIS], coeffs_ref[block], preferred_element_type=jnp.float32)
        )

    def project(owner, block):
        turned[...] = jnp.dot(
            pieces_ref[owner], rounded(geometry[block]), preferred_element_type=jnp.float32
        )

        def rows_of(step, carried):
            low = pl.multiple_of(step * 16, 16)
            half, inner = step // 3, pl.multiple_of(lax.rem(step, 3) * 16, 16)
            cosine, sine = turn(turned[pl.ds(low, 16), :])
            for polar in range(2):
                weight = turned[pl.ds(low + (polar + 1) * 2 * ROWS, 16), :]
                samples[polar * 2 + half, 0, pl.ds(inner, 16), :] = rounded(weight * cosine)
                samples[polar * 2 + half, 1, pl.ds(inner, 16), :] = rounded(weight * sine)
            return carried

        lax.fori_loop(0, 6, rows_of, 0)
        sums = lax.dot_general(
            samples[...].reshape(8 * ROWS, samples.shape[3]),
            coeffs_pad[block],
            (((1,), (1,)), ((), ())),
            preferred_element_type=jnp.float32,
        )
        for side in range(2):
            part[owner, block, side] = rounded(sums[:, side * 128 : side * 128 + 128]).reshape(
                RING, 2, ROWS, 128
            )

    across, after, before = along(x, 2), along(x, 1), along(x, 3)
    steps = [(block, side) for block in range(2) for side in range(2)]
    x_rings = [
        Ring(
            copies, x, x_peers[2], x_peers[0], lambda o, b=b, side=side: part.at[o, b, side],
            pl.ds(0, 2), pl.ds(2, 2), x_near.at[k], x_far.at[k],
        )
        for k, (b, side) in enumerate(steps)
    ]
    z_rings = [
        Ring(
            copies, z, z_peers[2], z_peers[0], lambda o, k=k: z_send.at[k, o],
            0, 1, z_near.at[k], z_far.at[k],
        )
        for k in range(4)
    ]
    z_direct = {}

    def cross(k):
        z_send[k] = rounded(x_rings[k].total())
        if ZRING:
            z_rings[k].step_1()
            return
        z_direct[k] = [
            copies.start(z_send.at[k, along(z, d)], z_far.at[k, d - 1], z_peers[d - 1]) for d in (2, 1, 3)
        ]

    def settle(k):
        block, side = steps[k]
        if ZRING:
            total = z_rings[k].total()
        else:
            for copy in z_direct[k]:
                copy.wait_recv()
            total = wide(z_send[k, z])
            for d in range(1, RING):
                total = total + wide(z_far[k, d - 1])
        pattern = rounded(total)
        mine = left.at[side, block, x, :, pl.ds(0, ROWS)]
        mine[...] = pattern
        for d in range(1, RING):
            copies.start(mine, mine, x_peers[d - 1], left_sems.at[side, block, x])
        held = jnp.concatenate([wide(pattern), jnp.zeros((2, HOLD - ROWS, 128), jnp.float32)], axis=1)
        turned_send[k] = rounded(jnp.transpose(held.reshape(2 * HOLD, 128))).reshape(2, HOLD, 2 * HOLD)
        for r in range(ROUND_TOTAL):
            for e in range(2):
                copies.start(
                    turned_send.at[k, e],
                    right.at[r, block, x],
                    other(r + 1, 2 * side + e),
                    right_sems.at[r, block, x],
                )

    prepare(0)
    project(across, 0)
    enter()
    x_rings[0].step_1()
    x_rings[1].step_1()
    prepare(1)
    project(across, 1)
    x_rings[2].step_1()
    x_rings[3].step_1()

    loads[4].wait()
    loads[5].wait()
    lobe_pair[0] = jnp.zeros((8, 128), jnp.float32)
    lobe_pair[0, 0:1, 0 : weights_ref.shape[1]] = weights_ref[...]
    lobe_pair[0, 1:2, 0 : weights_ref.shape[1]] = boost_ref[...]

    project(after, 0)
    project(before, 0)
    x_rings[0].step_2()
    x_rings[1].step_2()
    project(after, 1)
    project(before, 1)
    x_rings[2].step_2()
    x_rings[3].step_2()
    project(x, 0)
    project(x, 1)
    enter_z()
    paired = copies.start(lobe_pair.at[0], lobe_pair.at[1], z_pair)
    cross(0)
    enter_larger()
    cross(1)
    cross(2)
    if ZRING:
        z_rings[0].step_2()
    cross(3)
    if ZRING:
        z_rings[1].step_2()
    paired.wait_recv()
    lobe_all[x] = lobe_pair[...]
    for d in range(1, RING):
        copies.start(lobe_all.at[x], lobe_all.at[x], x_peers[d - 1], lobe_sems.at[x])
    if ZRING:
        z_rings[2].step_2()
    enter_smaller()
    settle(0)
    if ZRING:
        z_rings[3].step_2()
    settle(1)

    for load in loads[6:]:
        load.wait()
    row = lax.broadcasted_iota(jnp.int32, (8, 128), 0)
    flag_column = jnp.zeros((8, 128), jnp.float32)
    gaps = [jnp.zeros((8, 128), jnp.float32) for _ in range(3)]
    for k, (r, i, j) in enumerate(PAIRS):
        m = group * 2 + i
        n = lax.rem(group - r - 1 + groups, groups) * 2 + j
        flag_column = jnp.where(row == k, flags_ref[m, n].astype(jnp.float32), flag_column)
        for axis in range(3):
            gap = centers_ref[axis, m] - centers_ref[axis, n]
            gaps[axis] = jnp.where(row == k, gap, gaps[axis])
    odd = z_odd.astype(jnp.float32)
    below = lax.broadcasted_iota(jnp.int32, (128, 128), 0)
    sign = jnp.where(lax.broadcasted_iota(jnp.int32, (8, 128), 1) < HOLD, 1.0, -1.0)
    for d in range(1, RING):
        there = along(x, d)
        copies.arrive(lobe_all.at[there], lobe_sems.at[there], x_peers[d - 1])
    cosines, sines = [], []
    for source in range(RING):
        near = lobe_all[source, 0] * (1.0 - odd) + lobe_all[source, 1] * odd
        far = lobe_all[3 - source, 1] * (1.0 - odd) + lobe_all[3 - source, 0] * odd
        table = source * 2 + z_odd
        place = places_ref[table]
        sums = jnp.dot(
            near, jnp.where(below == place[0:1], 1.0, 0.0),
            precision=lax.Precision.HIGHEST, preferred_element_type=jnp.float32,
        ) + jnp.dot(
            far, jnp.where(below == place[1:2], 1.0, 0.0),
            precision=lax.Precision.HIGHEST, preferred_element_type=jnp.float32,
        )
        heading = headings_ref[table]
        cosine, sine = turn(heading[0:1] * gaps[0] + heading[1:2] * gaps[1] + heading[2:3] * gaps[2])
        amplitude = (sums[0:1] + flag_column * sums[1:2]) * (1.0 / math.sqrt(LOBE_TOTAL))
        cosines.append(amplitude * cosine)
        sines.append(amplitude * sine * sign)

    def couple(k):
        r, i, j = PAIRS[k]
        carries = []
        for source in range(RING):
            value = wide(right[r, j, source])
            carries.append(
                rounded(
                    cosines[source][k : k + 1] * value
                    + sines[source][k : k + 1] * pltpu.roll(value, HOLD, 1)
                )
            )
        carry = jnp.concatenate(carries, axis=1)
        total = jnp.concatenate(
            [
                jnp.dot(
                    carry, left[side, i].reshape(RING * 2 * HOLD, 128), preferred_element_type=jnp.float32
                )
                for side in range(2)
            ],
            axis=1,
        )
        total = jnp.dot(rounded(total), slabs[...], preferred_element_type=jnp.float32)
        zp[:, k] = rounded(total).reshape(RING, 16, LANES)

    def arrived_right(r, block):
        for source in range(RING):
            copies.arrive(right.at[r, block, source], right_sems.at[r, block, source], other(-r - 1, source))

    def arrived_left(block):
        for side in range(2):
            for d in range(1, RING):
                there = along(x, d)
                copies.arrive(
                    left.at[side, block, there, :, pl.ds(0, ROWS)],
                    left_sems.at[side, block, there],
                    x_peers[d - 1],
                )

    def scatter(parts):
        for p in parts:
            for k in range(*PARTS[p]):
                couple(k)
        for to_z in [1 - (z + 3) // 4, 3 - 2 * (z // 2), 2 + (z // 2) * (1 - z_odd)] if PRIO else [along(z, d) for d in (1,2,3)]:
            for p in parts:
                pairs = pl.ds(PARTS[p][0], PARTS[p][1] - PARTS[p][0])
                copies.start(zp.at[to_z, pairs], z_recv.at[z, pairs], at(to_z, x), z_sems.at[p, z])

    settle(2)
    settle(3)
    arrived_left(0)
    arrived_right(0, 0)
    arrived_right(1, 0)
    scatter([0])
    arrived_left(1)
    arrived_right(0, 1)
    arrived_right(1, 1)
    scatter([1, 2])

    back = []
    for p, (low, high) in enumerate(PARTS):
        pairs = pl.ds(low, high - low)
        total = wide(zp[z, pairs])
        for d in range(1, RING):
            there = along(z, d)
            copies.arrive(z_recv.at[there, pairs], z_sems.at[p, there], z_peers[d - 1])
            total = total + wide(z_recv[there, pairs])
        up_send[pairs] = rounded(total)
        for first, last in UPWARD[p]:
            mine = pl.ds(first, last - first)
            back.append(copies.start(up_send.at[mine], up_recv.at[mine], other(-PAIRS[first][0] - 1, x)))
        for k in range(low, high):
            r, i, j = PAIRS[k]
            lower_ref[i, r, :, j, :] = total[k - low, :SLAB, :BASIS]
    for copy in back:
        copy.wait_recv()
    for k, (r, i, j) in enumerate(PAIRS):
        upper_ref[j, r, :, i, :] = wide(up_recv[k])[:SLAB, :BASIS]
    copies.finish()


def shards(coeffs, offsets, moments, centers, near_flags, lobe_weights, near_boost):
    pieces, headings, places = grid_tables()
    unknowns = coeffs.shape[2]
    bf16, f32 = jnp.bfloat16, jnp.float32
    operands = (
        coeffs,
        jnp.transpose(offsets, (1, 0, 2)),
        jnp.transpose(moments, (1, 0, 2)),
        jnp.transpose(centers),
        near_flags,
        lobe_weights.reshape(1, -1),
        near_boost.reshape(1, -1),
        jnp.asarray(pieces),
        jnp.asarray(headings),
        jnp.asarray(places),
    )
    held = [pltpu.SMEM if k in (3, 4) else pltpu.VMEM for k in range(len(operands))]
    vmem = pl.BlockSpec(memory_space=pltpu.VMEM)
    out = pltpu.VMEM((2, ROUND_TOTAL, SLAB, 2, BASIS), f32)
    lower, upper = pl.pallas_call(
        kernel,
        out_shape=(out, out),
        in_specs=[pl.BlockSpec(memory_space=pltpu.HBM)] * len(operands),
        out_specs=(vmem, vmem),
        scratch_shapes=[
            *(space(operand.shape, operand.dtype) for space, operand in zip(held, operands)),
            pltpu.VMEM((LANES, LANES), bf16),
            pltpu.VMEM((2, DEPTH, unknowns), f32),
            pltpu.VMEM((2, LANES, unknowns), bf16),
            pltpu.VMEM((6 * ROWS, unknowns), f32),
            pltpu.VMEM((RING, 2, ROWS, unknowns), bf16),
            pltpu.VMEM((RING, 2, 2, RING, 2, ROWS, 128), bf16),
            pltpu.VMEM((4, 2, 2, 2, ROWS, 128), bf16),
            pltpu.VMEM((4, 2, RING, 2, ROWS, 128), bf16),
            pltpu.VMEM((4, RING, 2, ROWS, 128), bf16),
            pltpu.VMEM((4, 2, ROWS, 128), bf16),
            pltpu.VMEM((4, RING - 1, 2, ROWS, 128), bf16),
            pltpu.VMEM((2, 2, RING, 2, HOLD, 128), bf16),
            pltpu.VMEM((4, 2, HOLD, 2 * HOLD), bf16),
            pltpu.VMEM((ROUND_TOTAL, 2, RING, HOLD, 2 * HOLD), bf16),
            pltpu.VMEM((2, 8, 128), f32),
            pltpu.VMEM((RING, 2, 8, 128), f32),
            pltpu.VMEM((RING, 8, 16, LANES), bf16),
            pltpu.VMEM((RING, 8, 16, LANES), bf16),
            pltpu.VMEM((8, 16, LANES), bf16),
            pltpu.VMEM((8, 16, LANES), bf16),
            pltpu.SemaphoreType.DMA((N_COPIES,)),
            pltpu.SemaphoreType.DMA((N_COPIES,)),
            pltpu.SemaphoreType.DMA((2, 2, RING)),
            pltpu.SemaphoreType.DMA((ROUND_TOTAL, 2, RING)),
            pltpu.SemaphoreType.DMA((RING,)),
            pltpu.SemaphoreType.DMA((len(PARTS), RING)),
            pltpu.SemaphoreType.DMA((len(operands),)),
            pltpu.SemaphoreType.REGULAR,
            pltpu.SemaphoreType.REGULAR,
            pltpu.SemaphoreType.REGULAR,
        ],
        compiler_params=pltpu.CompilerParams(
            collective_id=0, has_side_effects=True, vmem_limit_bytes=48 * 1024 * 1024
        ),
        name="fill",
    )(*(pltpu.with_memory_space_constraint(operand, pltpu.HBM) for operand in operands))
    return jnp.transpose(lower, (0, 1, 3, 4, 2)), jnp.transpose(upper, (0, 1, 3, 2, 4))


def solution(mesh):
    placed = (
        P("grp", None, "sub"),
        P("grp", None, "sub"),
        P("grp", None, "sub"),
        P(),
        P(),
        P("sub"),
        P("sub"),
    )
    return jax.shard_map(
        shards,
        mesh=mesh,
        in_specs=placed,
        out_specs=(P("grp", None, None, None, "sub"), P("grp", None, None, "sub", None)),
        check_vma=False,
    )
```

```python
import math

import jax
import jax.numpy as jnp
import numpy as np
from jax import lax
from jax.experimental import pallas as pl
from jax.experimental.pallas import tpu as pltpu
from jax.sharding import PartitionSpec as P

THETAS = 20
PHIS = 36
DIRS = 720
LOBE_TOTAL = 1440
ROUND_TOTAL = 2
BASIS = 240
RING = 4
HALF = 45
ROWS = 48
HOLD = 64
SLAB = 15
LANES = 256
DEPTH = 32
MESH = pl.DeviceIdType.MESH
CENTER = 2


def heading_of(t):
    theta = np.pi * ((t // PHIS) + 0.5) / THETAS
    azimuth = 2.0 * np.pi * (t % PHIS) / PHIS
    st, ct, sa, ca = np.sin(theta), np.cos(theta), np.sin(azimuth), np.cos(azimuth)
    heading = np.stack([st * ca, st * sa, ct], axis=-1)
    along_theta = np.stack([ct * ca, ct * sa, -st], axis=-1)
    along_phi = np.stack([-sa, ca, np.zeros_like(sa)], axis=-1)
    return heading, along_theta, along_phi


def split3(value):
    value = value.astype(np.float32)
    parts = []
    for _ in range(3):
        part = value.astype(jnp.bfloat16)
        parts.append(part)
        value = value - part.astype(np.float32)
    return np.concatenate(parts, axis=-1)


def grid_tables():
    pieces = np.zeros((RING, 3, 2, ROWS, DEPTH), jnp.bfloat16)
    headings = np.zeros((2 * RING, 8, 2, HOLD), np.float32)
    places = np.full((2 * RING, 8, 2, HOLD), -1, np.int32)
    for xo in range(RING):
        for dh in range(2):
            t = 90 * xo + HALF * dh + np.arange(HALF)
            heading, along_theta, along_phi = heading_of(t)
            pieces[xo, 0, dh, :HALF, 0:9] = split3(0.5 * heading)
            pieces[xo, 1, dh, :HALF, 9:18] = split3(along_theta)
            pieces[xo, 2, dh, :HALF, 9:18] = split3(along_phi)
            headings[2 * xo + dh, 0:3, :, :HALF] = 0.5 * heading.T[:, None]
            opposite = PHIS * (THETAS - 1 - t // PHIS) + (t % PHIS + PHIS // 2) % PHIS - 90 * (7 - xo)
            assert opposite.min() >= 0 and opposite.max() < 90
            places[2 * xo + dh, 0, :, :HALF] = t - 90 * xo
            places[2 * xo + dh, 1, :, :HALF] = opposite
    wide_as = (2 * RING, 8, 2 * HOLD)
    return pieces.reshape(RING, 6 * ROWS, DEPTH), headings.reshape(wide_as), places.reshape(wide_as)


def turn_coefficients():
    nodes = np.cos(np.pi * (np.arange(400) + 0.5) / 400)
    square = 0.125 * (nodes + 1.0)
    r = np.sqrt(square)
    fit = np.polynomial.chebyshev.Chebyshev.fit
    cosine = fit(square, np.cos(2 * np.pi * r), 6, domain=[0, 0.25])
    sine = fit(square, -np.sin(2 * np.pi * r) / r, 5, domain=[0, 0.25])
    convert = np.polynomial.polynomial.Polynomial
    return (
        [float(v) for v in cosine.convert(kind=convert, domain=[-1, 1]).coef],
        [float(v) for v in sine.convert(kind=convert, domain=[-1, 1]).coef],
    )


COS_TERMS, SIN_TERMS = turn_coefficients()


def turn(s):
    r = s - jnp.round(s)
    y = r * r
    cosine = jnp.full_like(y, COS_TERMS[-1])
    for term in COS_TERMS[-2::-1]:
        cosine = cosine * y + term
    sine = jnp.full_like(y, SIN_TERMS[-1])
    for term in SIN_TERMS[-2::-1]:
        sine = sine * y + term
    return cosine, sine * r


def rounded(value):
    return value.astype(jnp.bfloat16)


def wide(value):
    return value.astype(jnp.float32)


class Copies:
    def __init__(self, send_sems, recv_sems):
        self.send_sems, self.recv_sems = send_sems, recv_sems
        self.all = []

    def start(self, source, target, device, arrival=None):
        place = len(self.all)
        copy = pltpu.make_async_remote_copy(
            src_ref=source,
            dst_ref=target,
            send_sem=self.send_sems.at[place],
            recv_sem=self.recv_sems.at[place] if arrival is None else arrival,
            device_id=device,
            device_id_type=MESH,
        )
        copy.start()
        self.all.append(copy)
        return copy

    def arrive(self, target, arrival, device):
        pltpu.make_async_remote_copy(
            src_ref=target,
            dst_ref=target,
            send_sem=self.send_sems.at[0],
            recv_sem=arrival,
            device_id=device,
            device_id_type=MESH,
        ).wait_recv()

    def finish(self):
        for copy in self.all:
            copy.wait_send()


class Ring:
    def __init__(self, copies, me, left, right, source, first, second, near, far):
        self.copies, self.left, self.right = copies, left, right
        self.across = source(lax.rem(me + 2, RING))
        self.after = source(lax.rem(me + 1, RING))
        self.before = source(lax.rem(me + 3, RING))
        self.own = source(me)
        self.first, self.second, self.near, self.far = first, second, near, far

    def step_1(self):
        self.from_left = self.copies.start(self.across.at[self.first], self.near.at[0], self.right)
        self.from_right = self.copies.start(self.across.at[self.second], self.near.at[1], self.left)

    def step_2(self):
        self.from_left.wait_recv()
        half = self.after.at[self.first]
        half[...] = rounded(wide(half[...]) + wide(self.near[0]))
        from_left = self.copies.start(self.after, self.far.at[0], self.right)
        self.from_right.wait_recv()
        half = self.before.at[self.second]
        half[...] = rounded(wide(half[...]) + wide(self.near[1]))
        from_right = self.copies.start(self.before, self.far.at[1], self.left)
        self.from_left, self.from_right = from_left, from_right

    def total(self):
        self.from_left.wait_recv()
        self.from_right.wait_recv()
        return wide(self.own[...]) + wide(self.far[0]) + wide(self.far[1])


PAIRS = [(0, 0, 0), (1, 0, 0), (0, 0, 1), (0, 1, 0), (0, 1, 1), (1, 0, 1), (1, 1, 0), (1, 1, 1)]
PARTS = [(0, 2), (2, 5), (5, 8)]
UPWARD = [[(0, 1), (1, 2)], [(2, 5)], [(5, 8)]]
N_COPIES = 4 + 4 * 4 + 4 * 4 + 4 * 3 + 4 * 4 + 3 * 3 + 4


def slab_matrix():
    place = lax.broadcasted_iota(jnp.int32, (LANES, LANES), 0)
    function = lax.broadcasted_iota(jnp.int32, (LANES, LANES), 1)
    x, z, i = place // 64, (place // 16) % RING, place % 16
    held = jnp.where(i < SLAB, SLAB * (z * RING + x) + i, -1)
    return jnp.where(held == function, 1.0, 0.0).astype(jnp.bfloat16)


def kernel(
    coeffs_hbm, offsets_hbm, moments_hbm, centers_hbm, flags_hbm, weights_hbm, boost_hbm,
    pieces_hbm, headings_hbm, places_hbm,
    both_ref,
    coeffs_ref, offsets_ref, moments_ref, centers_ref, flags_ref, weights_ref, boost_ref,
    pieces_ref, headings_ref, places_ref,
    slabs, geometry, coeffs_pad, turned, samples, part, x_near, x_far, z_send, z_near, z_far,
    left, turned_send, right, lobe_pair, lobe_all,
    zp, z_recv, up_send, up_recv,
    send_sems, recv_sems, left_sems, right_sems, lobe_sems, z_sems, load_sems, z_in, larger_in, smaller_in,
):
    group = lax.axis_index("grp")
    groups = lax.axis_size("grp")
    sub = lax.axis_index("sub")
    x, z = lax.rem(sub, RING), sub // RING
    z_odd = lax.rem(z, 2)

    def at(z_to, x_to):
        return {"sub": z_to * RING + x_to}

    def along(me, steps):
        return lax.rem(me + steps, RING)

    x_peers = [at(z, along(x, d)) for d in range(1, RING)]
    z_peers = [at(along(z, d), x) for d in range(1, RING)]
    z_pair = at(z + 1 - 2 * z_odd, x)

    def other(shift, x_to):
        return {"grp": lax.rem(group + shift + groups, groups), "sub": z * RING + x_to}

    left[:, :, :, :, ROWS:] = jnp.zeros((2, 2, RING, 2, HOLD - ROWS, 128), jnp.bfloat16)

    barrier = pltpu.get_barrier_semaphore()

    shifts = [(1, lax.rem(group + 1, groups)), (2, lax.rem(group + 2, groups))]
    shifts += [(-1, lax.rem(group + groups - 1, groups)), (-2, lax.rem(group + groups - 2, groups))]
    for peer in x_peers:
        pl.semaphore_signal(barrier, inc=1, device_id=peer, device_id_type=MESH)

    @pl.when(z != CENTER)
    def _():
        pl.semaphore_signal(barrier, inc=1, device_id=at(CENTER, x), device_id_type=MESH)

    smaller = 0
    for shift, place in shifts:
        smaller = smaller + jnp.where(place < group, 1, 0)

        @pl.when(group < place)
        def _(shift=shift):
            pl.semaphore_signal(barrier, inc=1, device_id=other(shift, x), device_id_type=MESH)

    greetings = RING - 1 + smaller + jnp.where(z == CENTER, RING - 1, 0)

    def enter():
        pl.semaphore_wait(barrier, greetings)

        @pl.when(z == CENTER)
        def _():
            for peer in z_peers:
                pl.semaphore_signal(z_in, inc=1, device_id=peer, device_id_type=MESH)

        for shift, place in shifts:

            @pl.when(place < group)
            def _(shift=shift):
                pl.semaphore_signal(larger_in, inc=1, device_id=other(shift, x), device_id_type=MESH)

    def enter_z():
        @pl.when(z != CENTER)
        def _():
            pl.semaphore_wait(z_in, 1)

    def enter_larger():
        @pl.when(smaller < 4)
        def _():
            pl.semaphore_wait(larger_in, 4 - smaller)

        for shift, place in shifts:

            @pl.when(group < place)
            def _(shift=shift):
                pl.semaphore_signal(smaller_in, inc=1, device_id=other(shift, x), device_id_type=MESH)

    def enter_smaller():
        @pl.when(smaller > 0)
        def _():
            pl.semaphore_wait(smaller_in, smaller)

    loads = [
        pltpu.make_async_copy(source, target, load_sems.at[k])
        for k, (source, target) in enumerate(
            [
                (offsets_hbm, offsets_ref),
                (moments_hbm, moments_ref),
                (pieces_hbm, pieces_ref),
                (coeffs_hbm, coeffs_ref),
                (weights_hbm, weights_ref),
                (boost_hbm, boost_ref),
                (centers_hbm, centers_ref),
                (flags_hbm, flags_ref),
                (headings_hbm, headings_ref),
                (places_hbm, places_ref),
            ]
        )
    ]
    for load in loads:
        load.start()

    copies = Copies(send_sems, recv_sems)
    slabs[...] = slab_matrix()
    for load in loads[:4]:
        load.wait()

    def prepare(block):
        geometry[block] = jnp.zeros((DEPTH, geometry.shape[2]), jnp.float32)
        for axis in range(3):
            offset = wide(offsets_ref[axis])[block : block + 1]
            moment = wide(moments_ref[axis])[block : block + 1]
            for piece in range(3):
                geometry[block, 3 * piece + axis : 3 * piece + axis + 1, :] = offset
                geometry[block, 9 + 3 * piece + axis : 10 + 3 * piece + axis, :] = moment
        coeffs_pad[block] = rounded(
            jnp.dot(slabs[:, :BASIS], coeffs_ref[block], preferred_element_type=jnp.float32)
        )

    def project(owner, block):
        turned[...] = jnp.dot(
            pieces_ref[owner], rounded(geometry[block]), preferred_element_type=jnp.float32
        )

        def rows_of(step, carried):
            low = pl.multiple_of(step * 16, 16)
            half, inner = step // 3, pl.multiple_of(lax.rem(step, 3) * 16, 16)
            cosine, sine = turn(turned[pl.ds(low, 16), :])
            for polar in range(2):
                weight = turned[pl.ds(low + (polar + 1) * 2 * ROWS, 16), :]
                samples[polar * 2 + half, 0, pl.ds(inner, 16), :] = rounded(weight * cosine)
                samples[polar * 2 + half, 1, pl.ds(inner, 16), :] = rounded(weight * sine)
            return carried

        lax.fori_loop(0, 6, rows_of, 0)
        sums = lax.dot_general(
            samples[...].reshape(8 * ROWS, samples.shape[3]),
            coeffs_pad[block],
            (((1,), (1,)), ((), ())),
            preferred_element_type=jnp.float32,
        )
        for side in range(2):
            part[owner, block, side] = rounded(sums[:, side * 128 : side * 128 + 128]).reshape(
                RING, 2, ROWS, 128
            )

    across, after, before = along(x, 2), along(x, 1), along(x, 3)
    steps = [(block, side) for block in range(2) for side in range(2)]
    x_rings = [
        Ring(
            copies, x, x_peers[2], x_peers[0], lambda o, b=b, side=side: part.at[o, b, side],
            pl.ds(0, 2), pl.ds(2, 2), x_near.at[k], x_far.at[k],
        )
        for k, (b, side) in enumerate(steps)
    ]
    z_rings = [
        Ring(
            copies, z, z_peers[2], z_peers[0], lambda o, k=k: z_send.at[k, o],
            0, 1, z_near.at[k], z_far.at[k],
        )
        for k in range(4)
    ]

    def cross(k):
        z_send[k] = rounded(x_rings[k].total())
        z_rings[k].step_1()

    def settle(k):
        block, side = steps[k]
        pattern = rounded(z_rings[k].total())
        mine = left.at[side, block, x, :, pl.ds(0, ROWS)]
        mine[...] = pattern
        for d in range(1, RING):
            copies.start(mine, mine, x_peers[d - 1], left_sems.at[side, block, x])
        held = jnp.concatenate([wide(pattern), jnp.zeros((2, HOLD - ROWS, 128), jnp.float32)], axis=1)
        turned_send[k] = rounded(jnp.transpose(held.reshape(2 * HOLD, 128))).reshape(2, HOLD, 2 * HOLD)
        for r in range(ROUND_TOTAL):
            for e in range(2):
                copies.start(
                    turned_send.at[k, e],
                    right.at[r, block, x],
                    other(r + 1, 2 * side + e),
                    right_sems.at[r, block, x],
                )

    prepare(0)
    project(across, 0)
    enter()
    x_rings[0].step_1()
    x_rings[1].step_1()
    prepare(1)
    project(across, 1)
    x_rings[2].step_1()
    x_rings[3].step_1()

    loads[4].wait()
    loads[5].wait()
    lobe_pair[0] = jnp.zeros((8, 128), jnp.float32)
    lobe_pair[0, 0:1, 0 : weights_ref.shape[1]] = weights_ref[...]
    lobe_pair[0, 1:2, 0 : weights_ref.shape[1]] = boost_ref[...]

    project(after, 0)
    project(before, 0)
    x_rings[0].step_2()
    x_rings[1].step_2()
    project(after, 1)
    project(before, 1)
    x_rings[2].step_2()
    x_rings[3].step_2()
    project(x, 0)
    project(x, 1)
    enter_z()
    paired = copies.start(lobe_pair.at[0], lobe_pair.at[1], z_pair)
    cross(0)
    enter_larger()
    cross(1)
    cross(2)
    z_rings[0].step_2()
    cross(3)
    z_rings[1].step_2()
    paired.wait_recv()
    lobe_all[x] = lobe_pair[...]
    for d in range(1, RING):
        copies.start(lobe_all.at[x], lobe_all.at[x], x_peers[d - 1], lobe_sems.at[x])
    z_rings[2].step_2()
    enter_smaller()
    settle(0)
    z_rings[3].step_2()
    settle(1)

    for load in loads[6:]:
        load.wait()
    row = lax.broadcasted_iota(jnp.int32, (8, 128), 0)
    flag_column = jnp.zeros((8, 128), jnp.float32)
    gaps = [jnp.zeros((8, 128), jnp.float32) for _ in range(3)]
    for k, (r, i, j) in enumerate(PAIRS):
        m = group * 2 + i
        n = lax.rem(group - r - 1 + groups, groups) * 2 + j
        flag_column = jnp.where(row == k, flags_ref[m, n].astype(jnp.float32), flag_column)
        for axis in range(3):
            gap = centers_ref[axis, m] - centers_ref[axis, n]
            gaps[axis] = jnp.where(row == k, gap, gaps[axis])
    odd = z_odd.astype(jnp.float32)
    below = lax.broadcasted_iota(jnp.int32, (128, 128), 0)
    sign = jnp.where(lax.broadcasted_iota(jnp.int32, (8, 128), 1) < HOLD, 1.0, -1.0)
    for d in range(1, RING):
        there = along(x, d)
        copies.arrive(lobe_all.at[there], lobe_sems.at[there], x_peers[d - 1])
    cosines, sines = [], []
    for source in range(RING):
        near = lobe_all[source, 0] * (1.0 - odd) + lobe_all[source, 1] * odd
        far = lobe_all[3 - source, 1] * (1.0 - odd) + lobe_all[3 - source, 0] * odd
        table = source * 2 + z_odd
        place = places_ref[table]
        sums = jnp.dot(
            near, jnp.where(below == place[0:1], 1.0, 0.0),
            precision=lax.Precision.HIGHEST, preferred_element_type=jnp.float32,
        ) + jnp.dot(
            far, jnp.where(below == place[1:2], 1.0, 0.0),
            precision=lax.Precision.HIGHEST, preferred_element_type=jnp.float32,
        )
        heading = headings_ref[table]
        cosine, sine = turn(heading[0:1] * gaps[0] + heading[1:2] * gaps[1] + heading[2:3] * gaps[2])
        amplitude = (sums[0:1] + flag_column * sums[1:2]) * (1.0 / math.sqrt(LOBE_TOTAL))
        cosines.append(amplitude * cosine)
        sines.append(amplitude * sine * sign)

    def couple(k):
        r, i, j = PAIRS[k]
        carries = []
        for source in range(RING):
            value = wide(right[r, j, source])
            carries.append(
                rounded(
                    cosines[source][k : k + 1] * value
                    + sines[source][k : k + 1] * pltpu.roll(value, HOLD, 1)
                )
            )
        carry = jnp.concatenate(carries, axis=1)
        total = jnp.concatenate(
            [
                jnp.dot(
                    carry, left[side, i].reshape(RING * 2 * HOLD, 128), preferred_element_type=jnp.float32
                )
                for side in range(2)
            ],
            axis=1,
        )
        total = jnp.dot(rounded(total), slabs[...], preferred_element_type=jnp.float32)
        zp[:, k] = rounded(total).reshape(RING, 16, LANES)

    def arrived_right(r, block):
        for source in range(RING):
            copies.arrive(right.at[r, block, source], right_sems.at[r, block, source], other(-r - 1, source))

    def arrived_left(block):
        for side in range(2):
            for d in range(1, RING):
                there = along(x, d)
                copies.arrive(
                    left.at[side, block, there, :, pl.ds(0, ROWS)],
                    left_sems.at[side, block, there],
                    x_peers[d - 1],
                )

    def scatter(parts):
        for p in parts:
            for k in range(*PARTS[p]):
                couple(k)
        for to_z in (1 - (z + 3) // 4, 3 - 2 * (z // 2), 2 + (z // 2) * (1 - z_odd)):
            for p in parts:
                pairs = pl.ds(PARTS[p][0], PARTS[p][1] - PARTS[p][0])
                copies.start(zp.at[to_z, pairs], z_recv.at[z, pairs], at(to_z, x), z_sems.at[p, z])

    settle(2)
    settle(3)
    arrived_left(0)
    arrived_right(0, 0)
    arrived_right(1, 0)
    scatter([0])
    arrived_left(1)
    arrived_right(0, 1)
    arrived_right(1, 1)
    scatter([1, 2])

    back = []
    for p, (low, high) in enumerate(PARTS):
        pairs = pl.ds(low, high - low)
        total = wide(zp[z, pairs])
        for d in range(1, RING):
            there = along(z, d)
            copies.arrive(z_recv.at[there, pairs], z_sems.at[p, there], z_peers[d - 1])
            total = total + wide(z_recv[there, pairs])
        up_send[pairs] = rounded(total)
        for first, last in UPWARD[p]:
            mine = pl.ds(first, last - first)
            back.append(copies.start(up_send.at[mine], up_recv.at[mine], other(-PAIRS[first][0] - 1, x)))
        for k in range(low, high):
            r, i, j = PAIRS[k]
            both_ref[0, i, r, :, j, :] = total[k - low, :SLAB, :BASIS]
    for copy in back:
        copy.wait_recv()
    for k, (r, i, j) in enumerate(PAIRS):
        both_ref[1, j, r, :, i, :] = wide(up_recv[k])[:SLAB, :BASIS]
    copies.finish()


def shards(coeffs, offsets, moments, centers, near_flags, lobe_weights, near_boost):
    pieces, headings, places = grid_tables()
    unknowns = coeffs.shape[2]
    bf16, f32 = jnp.bfloat16, jnp.float32
    operands = (
        coeffs,
        jnp.transpose(offsets, (1, 0, 2)),
        jnp.transpose(moments, (1, 0, 2)),
        jnp.transpose(centers),
        near_flags,
        lobe_weights.reshape(1, -1),
        near_boost.reshape(1, -1),
        jnp.asarray(pieces),
        jnp.asarray(headings),
        jnp.asarray(places),
    )
    held = [pltpu.SMEM if k in (3, 4) else pltpu.VMEM for k in range(len(operands))]
    vmem = pl.BlockSpec(memory_space=pltpu.VMEM)
    out = pltpu.VMEM((2, 2, ROUND_TOTAL, SLAB, 2, BASIS), f32)
    both = pl.pallas_call(
        kernel,
        out_shape=out,
        in_specs=[pl.BlockSpec(memory_space=pltpu.HBM)] * len(operands),
        out_specs=vmem,
        scratch_shapes=[
            *(space(operand.shape, operand.dtype) for space, operand in zip(held, operands)),
            pltpu.VMEM((LANES, LANES), bf16),
            pltpu.VMEM((2, DEPTH, unknowns), f32),
            pltpu.VMEM((2, LANES, unknowns), bf16),
            pltpu.VMEM((6 * ROWS, unknowns), f32),
            pltpu.VMEM((RING, 2, ROWS, unknowns), bf16),
            pltpu.VMEM((RING, 2, 2, RING, 2, ROWS, 128), bf16),
            pltpu.VMEM((4, 2, 2, 2, ROWS, 128), bf16),
            pltpu.VMEM((4, 2, RING, 2, ROWS, 128), bf16),
            pltpu.VMEM((4, RING, 2, ROWS, 128), bf16),
            pltpu.VMEM((4, 2, ROWS, 128), bf16),
            pltpu.VMEM((4, 2, 2, ROWS, 128), bf16),
            pltpu.VMEM((2, 2, RING, 2, HOLD, 128), bf16),
            pltpu.VMEM((4, 2, HOLD, 2 * HOLD), bf16),
            pltpu.VMEM((ROUND_TOTAL, 2, RING, HOLD, 2 * HOLD), bf16),
            pltpu.VMEM((2, 8, 128), f32),
            pltpu.VMEM((RING, 2, 8, 128), f32),
            pltpu.VMEM((RING, 8, 16, LANES), bf16),
            pltpu.VMEM((RING, 8, 16, LANES), bf16),
            pltpu.VMEM((8, 16, LANES), bf16),
            pltpu.VMEM((8, 16, LANES), bf16),
            pltpu.SemaphoreType.DMA((N_COPIES,)),
            pltpu.SemaphoreType.DMA((N_COPIES,)),
            pltpu.SemaphoreType.DMA((2, 2, RING)),
            pltpu.SemaphoreType.DMA((ROUND_TOTAL, 2, RING)),
            pltpu.SemaphoreType.DMA((RING,)),
            pltpu.SemaphoreType.DMA((len(PARTS), RING)),
            pltpu.SemaphoreType.DMA((len(operands),)),
            pltpu.SemaphoreType.REGULAR,
            pltpu.SemaphoreType.REGULAR,
            pltpu.SemaphoreType.REGULAR,
        ],
        compiler_params=pltpu.CompilerParams(
            collective_id=0, has_side_effects=True, vmem_limit_bytes=48 * 1024 * 1024
        ),
        name="fill",
    )(*(pltpu.with_memory_space_constraint(operand, pltpu.HBM) for operand in operands))
    lower, upper = both[0], both[1]
    return jnp.transpose(lower, (0, 1, 3, 4, 2)), jnp.transpose(upper, (0, 1, 3, 2, 4))


def solution(mesh):
    placed = (
        P("grp", None, "sub"),
        P("grp", None, "sub"),
        P("grp", None, "sub"),
        P(),
        P(),
        P("sub"),
        P("sub"),
    )
    return jax.shard_map(
        shards,
        mesh=mesh,
        in_specs=placed,
        out_specs=(P("grp", None, None, None, "sub"), P("grp", None, None, "sub", None)),
        check_vma=False,
    )
```

```python
import math

import jax
import jax.numpy as jnp
import numpy as np
from jax import lax
from jax.experimental import pallas as pl
from jax.experimental.pallas import tpu as pltpu
from jax.sharding import PartitionSpec as P

THETAS = 20
PHIS = 36
DIRS = 720
LOBE_TOTAL = 1440
ROUND_TOTAL = 2
BASIS = 240
RING = 4
HALF = 45
ROWS = 48
HOLD = 64
SLAB = 15
LANES = 256
DEPTH = 32
MESH = pl.DeviceIdType.MESH
CENTER = 2


def heading_of(t):
    theta = np.pi * ((t // PHIS) + 0.5) / THETAS
    azimuth = 2.0 * np.pi * (t % PHIS) / PHIS
    st, ct, sa, ca = np.sin(theta), np.cos(theta), np.sin(azimuth), np.cos(azimuth)
    heading = np.stack([st * ca, st * sa, ct], axis=-1)
    along_theta = np.stack([ct * ca, ct * sa, -st], axis=-1)
    along_phi = np.stack([-sa, ca, np.zeros_like(sa)], axis=-1)
    return heading, along_theta, along_phi


def split3(value):
    value = value.astype(np.float32)
    parts = []
    for _ in range(3):
        part = value.astype(jnp.bfloat16)
        parts.append(part)
        value = value - part.astype(np.float32)
    return np.concatenate(parts, axis=-1)


def grid_tables():
    pieces = np.zeros((RING, 3, 2, ROWS, DEPTH), jnp.bfloat16)
    headings = np.zeros((2 * RING, 8, 2, HOLD), np.float32)
    places = np.full((2 * RING, 8, 2, HOLD), -1, np.int32)
    for xo in range(RING):
        for dh in range(2):
            t = 90 * xo + HALF * dh + np.arange(HALF)
            heading, along_theta, along_phi = heading_of(t)
            pieces[xo, 0, dh, :HALF, 0:9] = split3(0.5 * heading)
            pieces[xo, 1, dh, :HALF, 9:18] = split3(along_theta)
            pieces[xo, 2, dh, :HALF, 9:18] = split3(along_phi)
            headings[2 * xo + dh, 0:3, :, :HALF] = 0.5 * heading.T[:, None]
            opposite = PHIS * (THETAS - 1 - t // PHIS) + (t % PHIS + PHIS // 2) % PHIS - 90 * (7 - xo)
            assert opposite.min() >= 0 and opposite.max() < 90
            places[2 * xo + dh, 0, :, :HALF] = t - 90 * xo
            places[2 * xo + dh, 1, :, :HALF] = opposite
    wide_as = (2 * RING, 8, 2 * HOLD)
    return pieces.reshape(RING, 6 * ROWS, DEPTH), headings.reshape(wide_as), places.reshape(wide_as)


def turn_coefficients():
    nodes = np.cos(np.pi * (np.arange(400) + 0.5) / 400)
    square = 0.125 * (nodes + 1.0)
    r = np.sqrt(square)
    fit = np.polynomial.chebyshev.Chebyshev.fit
    cosine = fit(square, np.cos(2 * np.pi * r), 6, domain=[0, 0.25])
    sine = fit(square, -np.sin(2 * np.pi * r) / r, 5, domain=[0, 0.25])
    convert = np.polynomial.polynomial.Polynomial
    return (
        [float(v) for v in cosine.convert(kind=convert, domain=[-1, 1]).coef],
        [float(v) for v in sine.convert(kind=convert, domain=[-1, 1]).coef],
    )


COS_TERMS, SIN_TERMS = turn_coefficients()


def turn(s):
    r = s - jnp.round(s)
    y = r * r
    cosine = jnp.full_like(y, COS_TERMS[-1])
    for term in COS_TERMS[-2::-1]:
        cosine = cosine * y + term
    sine = jnp.full_like(y, SIN_TERMS[-1])
    for term in SIN_TERMS[-2::-1]:
        sine = sine * y + term
    return cosine, sine * r


def rounded(value):
    return value.astype(jnp.bfloat16)


def wide(value):
    return value.astype(jnp.float32)


class Copies:
    def __init__(self, send_sems, recv_sems):
        self.send_sems, self.recv_sems = send_sems, recv_sems
        self.all = []

    def start(self, source, target, device, arrival=None):
        place = len(self.all)
        copy = pltpu.make_async_remote_copy(
            src_ref=source,
            dst_ref=target,
            send_sem=self.send_sems.at[place],
            recv_sem=self.recv_sems.at[place] if arrival is None else arrival,
            device_id=device,
            device_id_type=MESH,
        )
        copy.start()
        self.all.append(copy)
        return copy

    def arrive(self, target, arrival, device):
        pltpu.make_async_remote_copy(
            src_ref=target,
            dst_ref=target,
            send_sem=self.send_sems.at[0],
            recv_sem=arrival,
            device_id=device,
            device_id_type=MESH,
        ).wait_recv()

    def finish(self):
        for copy in self.all:
            copy.wait_send()


class Ring:
    def __init__(self, copies, me, left, right, source, first, second, near, far):
        self.copies, self.left, self.right = copies, left, right
        self.across = source(lax.rem(me + 2, RING))
        self.after = source(lax.rem(me + 1, RING))
        self.before = source(lax.rem(me + 3, RING))
        self.own = source(me)
        self.first, self.second, self.near, self.far = first, second, near, far

    def step_1(self):
        self.from_left = self.copies.start(self.across.at[self.first], self.near.at[0], self.right)
        self.from_right = self.copies.start(self.across.at[self.second], self.near.at[1], self.left)

    def step_2(self):
        self.from_left.wait_recv()
        half = self.after.at[self.first]
        half[...] = rounded(wide(half[...]) + wide(self.near[0]))
        from_left = self.copies.start(self.after, self.far.at[0], self.right)
        self.from_right.wait_recv()
        half = self.before.at[self.second]
        half[...] = rounded(wide(half[...]) + wide(self.near[1]))
        from_right = self.copies.start(self.before, self.far.at[1], self.left)
        self.from_left, self.from_right = from_left, from_right

    def total(self):
        self.from_left.wait_recv()
        self.from_right.wait_recv()
        return wide(self.own[...]) + wide(self.far[0]) + wide(self.far[1])


PAIRS = [(0, 0, 0), (1, 0, 0), (0, 0, 1), (0, 1, 0), (0, 1, 1), (1, 0, 1), (1, 1, 0), (1, 1, 1)]
PARTS = [(0, 2), (2, 5), (5, 8)]
UPWARD = [[(0, 1), (1, 2)], [(2, 5)], [(5, 8)]]
N_COPIES = 4 + 4 * 4 + 4 * 4 + 4 * 3 + 4 * 4 + 3 * 3 + 4


def slab_matrix():
    place = lax.broadcasted_iota(jnp.int32, (LANES, LANES), 0)
    function = lax.broadcasted_iota(jnp.int32, (LANES, LANES), 1)
    x, z, i = place // 64, (place // 16) % RING, place % 16
    held = jnp.where(i < SLAB, SLAB * (z * RING + x) + i, -1)
    return jnp.where(held == function, 1.0, 0.0).astype(jnp.bfloat16)


def kernel(
    coeffs_hbm, offsets_hbm, moments_hbm, centers_hbm, flags_hbm, weights_hbm, boost_hbm,
    pieces_hbm, headings_hbm, places_hbm,
    both_ref,
    coeffs_ref, offsets_ref, moments_ref, centers_ref, flags_ref, weights_ref, boost_ref,
    pieces_ref, headings_ref, places_ref,
    slabs, geometry, coeffs_pad, turned, samples, part, x_near, x_far, z_send, z_near, z_far,
    left, turned_send, right, lobe_pair, lobe_all,
    zp, z_recv, up_send, up_recv,
    send_sems, recv_sems, left_sems, right_sems, lobe_sems, z_sems, load_sems, z_in, larger_in, smaller_in,
):
    group = lax.axis_index("grp")
    groups = lax.axis_size("grp")
    sub = lax.axis_index("sub")
    x, z = lax.rem(sub, RING), sub // RING
    z_odd = lax.rem(z, 2)

    def at(z_to, x_to):
        return {"sub": z_to * RING + x_to}

    def along(me, steps):
        return lax.rem(me + steps, RING)

    x_peers = [at(z, along(x, d)) for d in range(1, RING)]
    z_peers = [at(along(z, d), x) for d in range(1, RING)]
    z_pair = at(z + 1 - 2 * z_odd, x)

    def other(shift, x_to):
        return {"grp": lax.rem(group + shift + groups, groups), "sub": z * RING + x_to}

    left[:, :, :, :, ROWS:] = jnp.zeros((2, 2, RING, 2, HOLD - ROWS, 128), jnp.bfloat16)

    barrier = pltpu.get_barrier_semaphore()

    shifts = [(1, lax.rem(group + 1, groups)), (2, lax.rem(group + 2, groups))]
    shifts += [(-1, lax.rem(group + groups - 1, groups)), (-2, lax.rem(group + groups - 2, groups))]
    for peer in x_peers:
        pl.semaphore_signal(barrier, inc=1, device_id=peer, device_id_type=MESH)

    @pl.when(z != CENTER)
    def _():
        pl.semaphore_signal(barrier, inc=1, device_id=at(CENTER, x), device_id_type=MESH)

    smaller = 0
    for shift, place in shifts:
        smaller = smaller + jnp.where(place < group, 1, 0)

        @pl.when(group < place)
        def _(shift=shift):
            pl.semaphore_signal(barrier, inc=1, device_id=other(shift, x), device_id_type=MESH)

    greetings = RING - 1 + smaller + jnp.where(z == CENTER, RING - 1, 0)

    def enter():
        pl.semaphore_wait(barrier, greetings)

        @pl.when(z == CENTER)
        def _():
            for peer in z_peers:
                pl.semaphore_signal(z_in, inc=1, device_id=peer, device_id_type=MESH)

        for shift, place in shifts:

            @pl.when(place < group)
            def _(shift=shift):
                pl.semaphore_signal(larger_in, inc=1, device_id=other(shift, x), device_id_type=MESH)

    def enter_z():
        @pl.when(z != CENTER)
        def _():
            pl.semaphore_wait(z_in, 1)

    def enter_larger():
        @pl.when(smaller < 4)
        def _():
            pl.semaphore_wait(larger_in, 4 - smaller)

        for shift, place in shifts:

            @pl.when(group < place)
            def _(shift=shift):
                pl.semaphore_signal(smaller_in, inc=1, device_id=other(shift, x), device_id_type=MESH)

    def enter_smaller():
        @pl.when(smaller > 0)
        def _():
            pl.semaphore_wait(smaller_in, smaller)

    loads = [
        pltpu.make_async_copy(source, target, load_sems.at[k])
        for k, (source, target) in enumerate(
            [
                (offsets_hbm, offsets_ref),
                (moments_hbm, moments_ref),
                (pieces_hbm, pieces_ref),
                (coeffs_hbm, coeffs_ref),
                (weights_hbm, weights_ref),
                (boost_hbm, boost_ref),
                (centers_hbm, centers_ref),
                (flags_hbm, flags_ref),
                (headings_hbm, headings_ref),
                (places_hbm, places_ref),
            ]
        )
    ]
    for load in loads:
        load.start()

    copies = Copies(send_sems, recv_sems)
    slabs[...] = slab_matrix()
    for load in loads[:4]:
        load.wait()

    def prepare(block):
        geometry[block] = jnp.zeros((DEPTH, geometry.shape[2]), jnp.float32)
        for axis in range(3):
            offset = wide(offsets_ref[axis])[block : block + 1]
            moment = wide(moments_ref[axis])[block : block + 1]
            for piece in range(3):
                geometry[block, 3 * piece + axis : 3 * piece + axis + 1, :] = offset
                geometry[block, 9 + 3 * piece + axis : 10 + 3 * piece + axis, :] = moment
        coeffs_pad[block] = rounded(
            jnp.dot(slabs[:, :BASIS], coeffs_ref[block], preferred_element_type=jnp.float32)
        )

    def project(owner, block):
        turned[...] = jnp.dot(
            pieces_ref[owner], rounded(geometry[block]), preferred_element_type=jnp.float32
        )

        def rows_of(step, carried):
            low = pl.multiple_of(step * 16, 16)
            half, inner = step // 3, pl.multiple_of(lax.rem(step, 3) * 16, 16)
            cosine, sine = turn(turned[pl.ds(low, 16), :])
            for polar in range(2):
                weight = turned[pl.ds(low + (polar + 1) * 2 * ROWS, 16), :]
                samples[polar * 2 + half, 0, pl.ds(inner, 16), :] = rounded(weight * cosine)
                samples[polar * 2 + half, 1, pl.ds(inner, 16), :] = rounded(weight * sine)
            return carried

        lax.fori_loop(0, 6, rows_of, 0)
        sums = lax.dot_general(
            samples[...].reshape(8 * ROWS, samples.shape[3]),
            coeffs_pad[block],
            (((1,), (1,)), ((), ())),
            preferred_element_type=jnp.float32,
        )
        for side in range(2):
            part[owner, block, side] = rounded(sums[:, side * 128 : side * 128 + 128]).reshape(
                RING, 2, ROWS, 128
            )

    across, after, before = along(x, 2), along(x, 1), along(x, 3)
    steps = [(block, side) for block in range(2) for side in range(2)]
    x_rings = [
        Ring(
            copies, x, x_peers[2], x_peers[0], lambda o, b=b, side=side: part.at[o, b, side],
            pl.ds(0, 2), pl.ds(2, 2), x_near.at[k], x_far.at[k],
        )
        for k, (b, side) in enumerate(steps)
    ]
    z_rings = [
        Ring(
            copies, z, z_peers[2], z_peers[0], lambda o, k=k: z_send.at[k, o],
            0, 1, z_near.at[k], z_far.at[k],
        )
        for k in range(4)
    ]

    def cross(k):
        z_send[k] = rounded(x_rings[k].total())
        z_rings[k].step_1()

    def settle(k):
        block, side = steps[k]
        pattern = rounded(z_rings[k].total())
        mine = left.at[side, block, x, :, pl.ds(0, ROWS)]
        mine[...] = pattern
        for d in range(1, RING):
            copies.start(mine, mine, x_peers[d - 1], left_sems.at[side, block, x])
        held = jnp.concatenate([wide(pattern), jnp.zeros((2, HOLD - ROWS, 128), jnp.float32)], axis=1)
        turned_send[k] = rounded(jnp.transpose(held.reshape(2 * HOLD, 128))).reshape(2, HOLD, 2 * HOLD)
        for r in range(ROUND_TOTAL):
            for e in range(2):
                copies.start(
                    turned_send.at[k, e],
                    right.at[r, block, x],
                    other(r + 1, 2 * side + e),
                    right_sems.at[r, block, x],
                )

    prepare(0)
    project(across, 0)
    enter()
    x_rings[0].step_1()
    x_rings[1].step_1()
    prepare(1)
    project(across, 1)
    x_rings[2].step_1()
    x_rings[3].step_1()

    loads[4].wait()
    loads[5].wait()
    lobe_pair[0] = jnp.zeros((8, 128), jnp.float32)
    lobe_pair[0, 0:1, 0 : weights_ref.shape[1]] = weights_ref[...]
    lobe_pair[0, 1:2, 0 : weights_ref.shape[1]] = boost_ref[...]

    project(after, 0)
    project(before, 0)
    project(after, 1)
    project(before, 1)
    x_rings[0].step_2()
    x_rings[1].step_2()
    x_rings[2].step_2()
    x_rings[3].step_2()
    project(x, 0)
    project(x, 1)
    enter_z()
    paired = copies.start(lobe_pair.at[0], lobe_pair.at[1], z_pair)
    cross(0)
    enter_larger()
    cross(1)
    cross(2)
    z_rings[0].step_2()
    cross(3)
    z_rings[1].step_2()
    paired.wait_recv()
    lobe_all[x] = lobe_pair[...]
    for d in range(1, RING):
        copies.start(lobe_all.at[x], lobe_all.at[x], x_peers[d - 1], lobe_sems.at[x])
    z_rings[2].step_2()
    enter_smaller()
    settle(0)
    z_rings[3].step_2()
    settle(1)

    for load in loads[6:]:
        load.wait()
    row = lax.broadcasted_iota(jnp.int32, (8, 128), 0)
    flag_column = jnp.zeros((8, 128), jnp.float32)
    gaps = [jnp.zeros((8, 128), jnp.float32) for _ in range(3)]
    for k, (r, i, j) in enumerate(PAIRS):
        m = group * 2 + i
        n = lax.rem(group - r - 1 + groups, groups) * 2 + j
        flag_column = jnp.where(row == k, flags_ref[m, n].astype(jnp.float32), flag_column)
        for axis in range(3):
            gap = centers_ref[axis, m] - centers_ref[axis, n]
            gaps[axis] = jnp.where(row == k, gap, gaps[axis])
    odd = z_odd.astype(jnp.float32)
    below = lax.broadcasted_iota(jnp.int32, (128, 128), 0)
    sign = jnp.where(lax.broadcasted_iota(jnp.int32, (8, 128), 1) < HOLD, 1.0, -1.0)
    for d in range(1, RING):
        there = along(x, d)
        copies.arrive(lobe_all.at[there], lobe_sems.at[there], x_peers[d - 1])
    cosines, sines = [], []
    for source in range(RING):
        near = lobe_all[source, 0] * (1.0 - odd) + lobe_all[source, 1] * odd
        far = lobe_all[3 - source, 1] * (1.0 - odd) + lobe_all[3 - source, 0] * odd
        table = source * 2 + z_odd
        place = places_ref[table]
        sums = jnp.dot(
            near, jnp.where(below == place[0:1], 1.0, 0.0),
            precision=lax.Precision.HIGHEST, preferred_element_type=jnp.float32,
        ) + jnp.dot(
            far, jnp.where(below == place[1:2], 1.0, 0.0),
            precision=lax.Precision.HIGHEST, preferred_element_type=jnp.float32,
        )
        heading = headings_ref[table]
        cosine, sine = turn(heading[0:1] * gaps[0] + heading[1:2] * gaps[1] + heading[2:3] * gaps[2])
        amplitude = (sums[0:1] + flag_column * sums[1:2]) * (1.0 / math.sqrt(LOBE_TOTAL))
        cosines.append(amplitude * cosine)
        sines.append(amplitude * sine * sign)

    def couple(k):
        r, i, j = PAIRS[k]
        carries = []
        for source in range(RING):
            value = wide(right[r, j, source])
            carries.append(
                rounded(
                    cosines[source][k : k + 1] * value
                    + sines[source][k : k + 1] * pltpu.roll(value, HOLD, 1)
                )
            )
        carry = jnp.concatenate(carries, axis=1)
        total = jnp.concatenate(
            [
                jnp.dot(
                    carry, left[side, i].reshape(RING * 2 * HOLD, 128), preferred_element_type=jnp.float32
                )
                for side in range(2)
            ],
            axis=1,
        )
        total = jnp.dot(rounded(total), slabs[...], preferred_element_type=jnp.float32)
        zp[:, k] = rounded(total).reshape(RING, 16, LANES)

    def arrived_right(r, block):
        for source in range(RING):
            copies.arrive(right.at[r, block, source], right_sems.at[r, block, source], other(-r - 1, source))

    def arrived_left(block):
        for side in range(2):
            for d in range(1, RING):
                there = along(x, d)
                copies.arrive(
                    left.at[side, block, there, :, pl.ds(0, ROWS)],
                    left_sems.at[side, block, there],
                    x_peers[d - 1],
                )

    def scatter(parts):
        for p in parts:
            for k in range(*PARTS[p]):
                couple(k)
        for to_z in (1 - (z + 3) // 4, 3 - 2 * (z // 2), 2 + (z // 2) * (1 - z_odd)):
            for p in parts:
                pairs = pl.ds(PARTS[p][0], PARTS[p][1] - PARTS[p][0])
                copies.start(zp.at[to_z, pairs], z_recv.at[z, pairs], at(to_z, x), z_sems.at[p, z])

    settle(2)
    settle(3)
    arrived_left(0)
    arrived_right(0, 0)
    arrived_right(1, 0)
    scatter([0])
    arrived_left(1)
    arrived_right(0, 1)
    arrived_right(1, 1)
    scatter([1, 2])

    back = []
    for p, (low, high) in enumerate(PARTS):
        pairs = pl.ds(low, high - low)
        total = wide(zp[z, pairs])
        for d in range(1, RING):
            there = along(z, d)
            copies.arrive(z_recv.at[there, pairs], z_sems.at[p, there], z_peers[d - 1])
            total = total + wide(z_recv[there, pairs])
        up_send[pairs] = rounded(total)
        for first, last in UPWARD[p]:
            mine = pl.ds(first, last - first)
            back.append(copies.start(up_send.at[mine], up_recv.at[mine], other(-PAIRS[first][0] - 1, x)))
        for k in range(low, high):
            r, i, j = PAIRS[k]
            both_ref[0, i, r, :, j, :] = total[k - low, :SLAB, :BASIS]
    for copy in back:
        copy.wait_recv()
    for k, (r, i, j) in enumerate(PAIRS):
        both_ref[1, j, r, :, i, :] = wide(up_recv[k])[:SLAB, :BASIS]
    copies.finish()


def shards(coeffs, offsets, moments, centers, near_flags, lobe_weights, near_boost):
    pieces, headings, places = grid_tables()
    unknowns = coeffs.shape[2]
    bf16, f32 = jnp.bfloat16, jnp.float32
    operands = (
        coeffs,
        jnp.transpose(offsets, (1, 0, 2)),
        jnp.transpose(moments, (1, 0, 2)),
        jnp.transpose(centers),
        near_flags,
        lobe_weights.reshape(1, -1),
        near_boost.reshape(1, -1),
        jnp.asarray(pieces),
        jnp.asarray(headings),
        jnp.asarray(places),
    )
    held = [pltpu.SMEM if k in (3, 4) else pltpu.VMEM for k in range(len(operands))]
    vmem = pl.BlockSpec(memory_space=pltpu.VMEM)
    out = pltpu.VMEM((2, 2, ROUND_TOTAL, SLAB, 2, BASIS), f32)
    both = pl.pallas_call(
        kernel,
        out_shape=out,
        in_specs=[pl.BlockSpec(memory_space=pltpu.HBM)] * len(operands),
        out_specs=vmem,
        scratch_shapes=[
            *(space(operand.shape, operand.dtype) for space, operand in zip(held, operands)),
            pltpu.VMEM((LANES, LANES), bf16),
            pltpu.VMEM((2, DEPTH, unknowns), f32),
            pltpu.VMEM((2, LANES, unknowns), bf16),
            pltpu.VMEM((6 * ROWS, unknowns), f32),
            pltpu.VMEM((RING, 2, ROWS, unknowns), bf16),
            pltpu.VMEM((RING, 2, 2, RING, 2, ROWS, 128), bf16),
            pltpu.VMEM((4, 2, 2, 2, ROWS, 128), bf16),
            pltpu.VMEM((4, 2, RING, 2, ROWS, 128), bf16),
            pltpu.VMEM((4, RING, 2, ROWS, 128), bf16),
            pltpu.VMEM((4, 2, ROWS, 128), bf16),
            pltpu.VMEM((4, 2, 2, ROWS, 128), bf16),
            pltpu.VMEM((2, 2, RING, 2, HOLD, 128), bf16),
            pltpu.VMEM((4, 2, HOLD, 2 * HOLD), bf16),
            pltpu.VMEM((ROUND_TOTAL, 2, RING, HOLD, 2 * HOLD), bf16),
            pltpu.VMEM((2, 8, 128), f32),
            pltpu.VMEM((RING, 2, 8, 128), f32),
            pltpu.VMEM((RING, 8, 16, LANES), bf16),
            pltpu.VMEM((RING, 8, 16, LANES), bf16),
            pltpu.VMEM((8, 16, LANES), bf16),
            pltpu.VMEM((8, 16, LANES), bf16),
            pltpu.SemaphoreType.DMA((N_COPIES,)),
            pltpu.SemaphoreType.DMA((N_COPIES,)),
            pltpu.SemaphoreType.DMA((2, 2, RING)),
            pltpu.SemaphoreType.DMA((ROUND_TOTAL, 2, RING)),
            pltpu.SemaphoreType.DMA((RING,)),
            pltpu.SemaphoreType.DMA((len(PARTS), RING)),
            pltpu.SemaphoreType.DMA((len(operands),)),
            pltpu.SemaphoreType.REGULAR,
            pltpu.SemaphoreType.REGULAR,
            pltpu.SemaphoreType.REGULAR,
        ],
        compiler_params=pltpu.CompilerParams(
            collective_id=0, has_side_effects=True, vmem_limit_bytes=48 * 1024 * 1024
        ),
        name="fill",
    )(*(pltpu.with_memory_space_constraint(operand, pltpu.HBM) for operand in operands))
    lower, upper = both[0], both[1]
    return jnp.transpose(lower, (0, 1, 3, 4, 2)), jnp.transpose(upper, (0, 1, 3, 2, 4))


def solution(mesh):
    placed = (
        P("grp", None, "sub"),
        P("grp", None, "sub"),
        P("grp", None, "sub"),
        P(),
        P(),
        P("sub"),
        P("sub"),
    )
    return jax.shard_map(
        shards,
        mesh=mesh,
        in_specs=placed,
        out_specs=(P("grp", None, None, None, "sub"), P("grp", None, None, "sub", None)),
        check_vma=False,
    )
```
